256 devices in a mesh: row: 8 (over y, x_hi), col: 32 (over z, x_lo, core).
Axes of the slice: x: 4 (x_hi: 2, x_lo: 2; x = x_hi * 2 + x_lo), y: 4, z: 8, core: 2. Of those that a mesh axis runs over, the one named last changes fastest.
Arguments:
- covariance: float32 [12288, 12288], P('row', 'col'), may hold values from -6 to 6
- process_noise: float32 [12288, 12288], P('row', 'col'), may hold values from -3 to 3
- depth_field: float32 [64, 64], replicated, may hold values from 0.4 to 2
- coriolis: float32 [64, 64], replicated, may hold values from -0.6 to 0.6
- drag_rate: float32 [64, 64], replicated, may hold values from 0.05 to 0.5
Outputs:
- forecast: float32 [12288, 12288], P('row', 'col')
The draws below stay inside these ranges and needn't reach their ends.
All inputs are finite; a program needn't handle non-finite values.
Results may differ from the reference program's by a relative error of at most 0.00002.
Values sent between devices are 32-bit elements; how exact they have to be, the bound alone decides.
No kernel may reach another device: no remote copies, remote signals or barrier semaphores. Data moves between devices by JAX's collectives and lax.ppermute only.
A program may use at most 128 MiB of HBM per device.

```python
import math
import jax
import jax.numpy as jnp
from jax import lax

GX = 64
GY = 64
STATE = 12288


def steps_of(own_key, dims, split, smallest, high):
    level, own = 1.0, jax.random.fold_in(own_key, 6)
    for axis_at, blocks in split:
        steps = jnp.exp(jax.random.uniform(jax.random.fold_in(own, axis_at), (blocks,), jnp.float32, smallest / len(split), high / len(split)))
        level = level * jnp.repeat(steps, dims[axis_at] // blocks).reshape([-1 if axis == axis_at else 1 for axis in range(len(dims))])
    return level


def scatter_about(key, dims, deviation, limit, pieces=(), kind=jnp.bfloat16):
    drawn = deviation * jax.random.normal(key, dims, jnp.float32)
    if pieces:
        drawn = drawn * steps_of(key, dims, pieces, -0.22, 0.18)
    return jnp.clip(drawn, -limit, limit).astype(kind)


def setup_inputs(seed: int = 0) -> dict:
    arg_keys = jax.random.split(jax.random.key(seed), 6)
    return {
        "covariance": scatter_about(arg_keys[0], (STATE, STATE), 1.0, 6.0, ((0, 8), (1, 32)), jnp.float32),
        "process_noise": scatter_about(arg_keys[1], (STATE, STATE), 0.5, 3.0, ((0, 8), (1, 32)), jnp.float32),
        "depth_field": jnp.clip(jnp.exp(jax.random.uniform(arg_keys[2], (GY, GX), jnp.float32, math.log(0.4), math.log(2.0))), 0.4, 2.0),
        "coriolis": jnp.clip(jax.random.uniform(arg_keys[3], (GY, GX), jnp.float32, -0.6, 0.6), -0.6, 0.6),
        "drag_rate": jnp.clip(jnp.exp(jax.random.uniform(arg_keys[4], (GY, GX), jnp.float32, math.log(0.05), math.log(0.5))), 0.05, 0.5),
    }


STEP_SIZE = 0.9


def x_diff(field):
    padded = jnp.pad(field, ((0, 0), (1, 1), (0, 0)))
    return padded[:, 2:] - padded[:, :-2]


def tendency(padded, depth_rows, coriolis_rows, drag_rows):
    inner = padded[1:-1]
    height = inner[:, 0]
    east_flow = inner[:, 1]
    north_flow = inner[:, 2]
    depth_b = depth_rows[:, :, None]
    turn_b = coriolis_rows[:, :, None]
    drag_b = drag_rows[:, :, None]
    d_height = -0.5 * depth_b * (x_diff(east_flow) + (padded[2:, 2] - padded[:-2, 2]))
    d_east = -0.5 * x_diff(height) + turn_b * north_flow - drag_b * east_flow
    d_north = -0.5 * (padded[2:, 0] - padded[:-2, 0]) - turn_b * east_flow - drag_b * north_flow
    return jnp.stack([d_height, d_east, d_north], axis=1)


def advance(field, extend, depth_rows, coriolis_rows, drag_rows):
    slope_one = tendency(extend(field), depth_rows, coriolis_rows, drag_rows)
    slope_two = tendency(extend(field + (0.5 * STEP_SIZE) * slope_one), depth_rows, coriolis_rows, drag_rows)
    slope_three = tendency(extend(field + (0.5 * STEP_SIZE) * slope_two), depth_rows, coriolis_rows, drag_rows)
    slope_four = tendency(extend(field + STEP_SIZE * slope_three), depth_rows, coriolis_rows, drag_rows)
    return field + (STEP_SIZE / 6.0) * (slope_one + 2.0 * slope_two + 2.0 * slope_three + slope_four)


def pad_rows(field):
    return jnp.pad(field, ((1, 1), (0, 0), (0, 0), (0, 0)))


def propagate(matrix, depth_field, coriolis, drag_rate):
    block_cols = 3 * GX
    count = STATE // block_cols
    blocks = matrix.reshape(STATE, count, block_cols).transpose(1, 0, 2)

    def one_block(block):
        field = block.reshape(GY, 3, GX, block_cols)
        moved = advance(field, pad_rows, depth_field, coriolis, drag_rate)
        return moved.reshape(STATE, block_cols)

    moved_blocks = lax.map(one_block, blocks)
    return moved_blocks.transpose(1, 0, 2).reshape(STATE, STATE)


def reference(covariance, process_noise, depth_field, coriolis, drag_rate):
    forward = propagate(covariance, depth_field, coriolis, drag_rate)
    twice = propagate(forward.T, depth_field, coriolis, drag_rate)
    return twice.T + process_noise
```

```python
import functools

import jax
import jax.numpy as jnp
from jax import lax
from jax.experimental import pallas as pl
from jax.experimental.pallas import tpu as pltpu
from jax.sharding import PartitionSpec as P

GX = 64
STEP = 0.9
SEG = 72
LANES = 128
CHUNKS = 2
D, F, R, B = 0, 1, 2, 3
MIB = 1024 * 1024


def at(row, comp):
    return (row * 3 + comp) * SEG + 8


def buffer_rows(rows):
    return rows * 3 * SEG + 8


def zero_gaps(ref, rows):
    for i in range(rows * 3 + 1):
        ref[pl.ds(i * SEG, 8), :] = jnp.zeros((8, LANES), jnp.float32)


def load_coefficients(dep_ref, cor_ref, drag_ref, first, count, coef_ref, slot_of=None, turn=None):
    shift = lax.rem(128 - first + 128, 128)
    lane = lax.broadcasted_iota(jnp.int32, (GX, LANES), 1)
    inside = jnp.where(lane < GX, 1.0, 0.0).astype(jnp.float32)

    def rolled(ref, scale):
        wide = jnp.concatenate([ref[...].T, jnp.zeros((GX, LANES - GX), jnp.float32)], axis=1)
        return pltpu.roll(wide * scale, shift, 1)

    tables = {
        D: rolled(dep_ref, -0.5 * STEP),
        F: rolled(cor_ref, STEP),
        R: rolled(drag_ref, STEP),
        B: pltpu.roll(inside * (-0.5 * STEP), shift, 1),
    }
    if turn is not None:
        tables[F] = tables[F] * turn
    for j in range(count):
        slot = j if slot_of is None else slot_of(j)
        for kind, table in tables.items():
            coef_ref[slot, kind] = jnp.broadcast_to(table[:, j : j + 1], (GX, LANES))


def total(terms):
    terms = [t for t in terms if t is not None]
    if not terms:
        return None
    acc = terms[0]
    for t in terms[1:]:
        acc = acc + t
    return acc


def tendency(src, have, row, base, coef, slot, ghost=False, want=(0, 1, 2), turn=1):
    def get(r, c, shift=0):
        return src[pl.ds(at(r + base, c) + shift, GX), :]

    def diff_x(c):
        return get(row, c, 1) - get(row, c, -1)

    def diff_y(c):
        above, below = (row + 1, c) in have, (row - 1, c) in have
        if above and below:
            return get(row + 1, c) - get(row - 1, c)
        if above:
            return get(row + 1, c)
        if below:
            return -get(row - 1, c)
        return None

    half = coef[slot, B] if ghost else jnp.float32(-0.5 * STEP)
    center = [get(row, c) if (row, c) in have else None for c in range(3)]
    out = {}
    if 0 in want:
        s = total([diff_x(1) if center[1] is not None else None, diff_y(2)])
        out[0] = None if s is None else coef[slot, D] * s
    if 1 in want:
        dx = half * diff_x(0) if center[0] is not None else None
        spin = None if center[2] is None else (turn * coef[slot, F] if turn != 1 else coef[slot, F]) * center[2]
        drag = None if center[1] is None else -(coef[slot, R] * center[1])
        out[1] = total([dx, spin, drag])
    if 2 in want:
        dy = diff_y(0)
        dy = None if dy is None else half * dy
        spin = None if center[1] is None else (-turn * coef[slot, F]) * center[1]
        drag = None if center[2] is None else -(coef[slot, R] * center[2])
        out[2] = total([dy, spin, drag])
    return out


def powers(bufs, rows, base, coef, finish):
    have = {(r, c) for r in range(rows) for c in range(3)}
    for j, reach in ((1, 1), (2, 2), (3, 1)):
        new = set()
        for r in range(-reach, rows + reach):
            ghost = r < 0 or r >= rows
            want = (0, 2) if ghost and j == 3 else (0, 1, 2)
            out = tendency(bufs[j - 1], have, r, base, coef, r + 2, ghost, want)
            for c, v in out.items():
                if v is not None:
                    bufs[j][pl.ds(at(r + base, c), GX), :] = v if j == 1 else v * (1.0 / j)
                    new.add((r, c))
        have = new
    for r in range(rows):
        out = tendency(bufs[3], have, r, base, coef, r + 2)
        for c in range(3):
            finish(r, c, out[c] * 0.25)


FACT = [1.0, 1.0, 2.0, 6.0, 24.0]


def response(message, bufs, base, coef, slot_of, finish, turn=1):
    heights = [message(j, 0) for j in range(4)]
    norths = [message(j, 1) for j in range(4)]
    forces = []
    for m in range(4):
        weights = [FACT[j] / FACT[j + 1 + m] for j in range(4 - m)]
        fh = total([w * heights[j] for j, w in enumerate(weights)])
        fn = total([w * norths[j] for j, w in enumerate(weights)])
        forces.append((-(coef[slot_of(0), D] * fn), (0.5 * STEP) * fh))
    have = set()
    src = None
    for step, m in enumerate((3, 2, 1, 0)):
        new = set()
        for d in range(step + 1):
            out = {0: None, 1: None, 2: None}
            if src is not None:
                out = tendency(src, have, d, base, coef, slot_of(d), turn=turn)
            if d == 0:
                out[0] = total([out[0], forces[m][0]])
                out[2] = total([out[2], forces[m][1]])
            for c, v in out.items():
                if m == 0:
                    finish(d, c, v)
                elif v is not None:
                    bufs[step % 2][pl.ds(at(d + base, c), GX), :] = v
                    new.add((d, c))
        have, src = new, bufs[step % 2]


def rows_kernel(scal, x_ref, dep, cor, drag, s00, s01, s10, s11, b0, b1, coef, v0, v1, v2, v3, acc, top, bottom):
    rows, base = 8, 2

    @pl.when(pl.program_id(0) == 0)
    def _():
        load_coefficients(dep, cor, drag, scal[0] - 2, rows + 4, coef)
        for ref in (v0, v1, v2, v3):
            zero_gaps(ref, rows + 4)

    for r in range(rows):
        for c in range(3):
            v0[pl.ds(at(r + base, c), GX), :] = x_ref[pl.ds((r * 3 + c) * GX, GX), :]

    def finish(r, c, v4):
        place = r if r < 4 else 4 + (7 - r)
        i = at(r + base, c)
        v = v4 + v3[pl.ds(i, GX), :] + v2[pl.ds(i, GX), :] + v1[pl.ds(i, GX), :] + v0[pl.ds(i, GX), :]
        acc[pl.ds((place * 3 + c) * GX, GX), :] = v

    powers((v0, v1, v2, v3), rows, base, coef, finish)
    for j, ref in enumerate((v0, v1, v2, v3)):
        for i, c in enumerate((0, 2)):
            top[pl.ds((j * 2 + i) * GX, GX), :] = ref[pl.ds(at(base, c), GX), :]
            bottom[pl.ds((j * 2 + i) * GX, GX), :] = ref[pl.ds(at(rows - 1 + base, c), GX), :]

    half, part = 768, 768 // CHUNKS
    core = scal[1]

    @pl.when(core == 0)
    def _():
        s00[...] = acc[pl.ds(0, part), :]
        s01[...] = acc[pl.ds(part, part), :]
        s10[...] = acc[pl.ds(half, part), :]
        s11[...] = acc[pl.ds(half + part, part), :]
        b0[...] = bottom[...]
        b1[...] = top[...]

    @pl.when(core == 1)
    def _():
        s10[...] = acc[pl.ds(0, part), :]
        s11[...] = acc[pl.ds(part, part), :]
        s00[...] = acc[pl.ds(half, part), :]
        s01[...] = acc[pl.ds(half + part, part), :]
        b1[...] = bottom[...]
        b0[...] = top[...]


def whole(ref_shape):
    return pl.BlockSpec(ref_shape, lambda i, *_: tuple(0 for _ in ref_shape))


def vmem(rows, cols=LANES):
    return pltpu.VMEM((rows, cols), jnp.float32)


def shape(rows, cols):
    return jax.ShapeDtypeStruct((rows, cols), jnp.float32)


def params(mib):
    return pltpu.CompilerParams(vmem_limit_bytes=mib * MIB)


def lane_block(rows):
    return pl.BlockSpec((rows, LANES), lambda i, *_: (0, i))


def rows_step(scal, block, fields):
    table = whole((GX, GX))
    part = 768 // CHUNKS
    buf = vmem(buffer_rows(12))
    return pl.pallas_call(
        rows_kernel,
        grid_spec=pltpu.PrefetchScalarGridSpec(
            num_scalar_prefetch=1,
            grid=(3,),
            in_specs=[lane_block(1536), table, table, table],
            out_specs=[lane_block(part)] * 4 + [lane_block(512)] * 2,
            scratch_shapes=[pltpu.VMEM((12, 4, GX, LANES), jnp.float32), buf, buf, buf, buf, vmem(1536), vmem(512), vmem(512)],
        ),
        out_shape=[shape(part, 384)] * 4 + [shape(512, 384)] * 2,
        compiler_params=params(24),
        name="rows_step",
    )(scal, block, *fields)


def rows_response_kernel(scal, m0, m1, dep, cor, drag, r0, r1, coef, t0, t1):
    half = scal[1]
    turn = 1.0 - 2.0 * half.astype(jnp.float32)

    @pl.when(pl.program_id(0) == 0)
    def _():
        load_coefficients(dep, cor, drag, scal[0], 4, coef, lambda j: jnp.where(half == 0, j, 3 - j), turn)
        for ref in (t0, t1):
            zero_gaps(ref, 4)

    for m_ref, r_ref in ((m0, r0), (m1, r1)):

        def message(j, i, m_ref=m_ref):
            v = m_ref[pl.ds((j * 2 + i) * GX, GX), :]
            return v * turn if i == 1 else v

        def finish(d, c, v, r_ref=r_ref):
            v = jnp.zeros((GX, LANES), jnp.float32) if v is None else v
            r_ref[pl.ds((d * 3 + c) * GX, GX), :] = v * turn if c == 2 else v

        response(message, (t0, t1), 0, coef, lambda d: d, finish)


def rows_response(scal, m0, m1, fields):
    table = whole((GX, GX))
    buf = vmem(buffer_rows(4))
    return pl.pallas_call(
        rows_response_kernel,
        grid_spec=pltpu.PrefetchScalarGridSpec(
            num_scalar_prefetch=1,
            grid=(3,),
            in_specs=[lane_block(512)] * 2 + [table] * 3,
            out_specs=[lane_block(768)] * 2,
            scratch_shapes=[pltpu.VMEM((4, 4, GX, LANES), jnp.float32), buf, buf],
        ),
        out_shape=[shape(768, 384)] * 2,
        compiler_params=params(16),
        name="rows_response",
    )(scal, m0, m1, *fields)


def columns_kernel(scal, s0, s1, r0, r1, dep, cor, drag, out, left, right, coef, v0, v1, v2, v3):
    rows, base = 4, 2
    half = scal[1]

    @pl.when(pl.program_id(0) == 0)
    def _():
        load_coefficients(dep, cor, drag, scal[0] - 2, rows + 4, coef)
        for ref in (v0, v1, v2, v3):
            zero_gaps(ref, rows + 4)

    for k, (s_ref, r_ref) in enumerate(((s0, r0), (s1, r1))):
        core = half if k == 0 else 1 - half
        start = pl.multiple_of(core * (2 * 3 * SEG), 8)
        for t in range(3):
            piece = (s_ref[:, t * LANES : (t + 1) * LANES] + r_ref[:, t * LANES : (t + 1) * LANES]).T
            for i in range(2):
                seg = t * 2 + i
                place = pl.multiple_of(start + (base * 3 + seg) * SEG + 8, 8)
                v0[pl.ds(place, GX), :] = piece[i * GX : (i + 1) * GX, :]

    def finish(r, c, v4):
        i = at(r + base, c)
        v = v4 + v3[pl.ds(i, GX), :] + v2[pl.ds(i, GX), :] + v1[pl.ds(i, GX), :] + v0[pl.ds(i, GX), :]
        out[pl.ds((r * 3 + c) * GX, GX), :] = v

    powers((v0, v1, v2, v3), rows, base, coef, finish)
    for j, ref in enumerate((v0, v1, v2, v3)):
        for i, c in enumerate((0, 2)):
            left[pl.ds((j * 2 + i) * GX, GX), :] = ref[pl.ds(at(base, c), GX), :]
            right[pl.ds((j * 2 + i) * GX, GX), :] = ref[pl.ds(at(rows - 1 + base, c), GX), :]


def columns_step(scal, s0, s1, r0, r1, fields, chunk):
    table = whole((GX, GX))
    part = 768 // CHUNKS
    tiles = part // LANES
    buf = vmem(buffer_rows(8))
    return pl.pallas_call(
        columns_kernel,
        grid_spec=pltpu.PrefetchScalarGridSpec(
            num_scalar_prefetch=1,
            grid=(tiles,),
            in_specs=[pl.BlockSpec((LANES, 384), lambda i, *_: (i, 0))] * 2
            + [pl.BlockSpec((LANES, 384), lambda i, *_: (i + chunk * tiles, 0))] * 2
            + [table] * 3,
            out_specs=[lane_block(768), lane_block(512), lane_block(512)],
            scratch_shapes=[pltpu.VMEM((8, 4, GX, LANES), jnp.float32), buf, buf, buf, buf],
        ),
        out_shape=[shape(768, part), shape(512, part), shape(512, part)],
        compiler_params=params(24),
        name="columns_step",
    )(scal, s0, s1, r0, r1, *fields)


def columns_response_kernel(scal, own, from_left, from_right, dep, cor, drag, z0, z1, coef, t0, t1, acc):
    half = scal[1]

    @pl.when(pl.program_id(0) == 0)
    def _():
        load_coefficients(dep, cor, drag, scal[0], 4, coef)
        for ref in (t0, t1):
            zero_gaps(ref, 4)

    def message_left(j, i):
        return from_left[pl.ds((j * 2 + i) * GX, GX), :]

    def finish_left(d, c, v):
        i = pl.ds((d * 3 + c) * GX, GX)
        acc[i, :] = own[i, :] if v is None else own[i, :] + v

    response(message_left, (t0, t1), 0, coef, lambda d: d, finish_left)

    def message_right(j, i):
        v = from_right[pl.ds((j * 2 + i) * GX, GX), :]
        return -v if i == 1 else v

    def finish_right(d, c, v):
        i = pl.ds(((3 - d) * 3 + c) * GX, GX)
        if v is not None:
            acc[i, :] = acc[i, :] + (-v if c == 2 else v)

    response(message_right, (t0, t1), 0, coef, lambda d: 3 - d, finish_right, turn=-1)
    for k, z_ref in enumerate((z0, z1)):
        core = half if k == 0 else 1 - half
        for t in range(3):
            place = pl.multiple_of(core * 384 + t * LANES, LANES)
            z_ref[:, t * LANES : (t + 1) * LANES] = acc[pl.ds(place, LANES), :].T


def columns_response(scal, own, from_left, from_right, fields):
    table = whole((GX, GX))
    part = 768 // CHUNKS
    buf = vmem(buffer_rows(4))
    return pl.pallas_call(
        columns_response_kernel,
        grid_spec=pltpu.PrefetchScalarGridSpec(
            num_scalar_prefetch=1,
            grid=(part // LANES,),
            in_specs=[lane_block(768), lane_block(512), lane_block(512)] + [table] * 3,
            out_specs=[pl.BlockSpec((LANES, 384), lambda i, *_: (i, 0))] * 2,
            scratch_shapes=[pltpu.VMEM((4, 4, GX, LANES), jnp.float32), buf, buf, vmem(768)],
        ),
        out_shape=[shape(part, 384)] * 2,
        compiler_params=params(16),
        name="columns_response",
    )(scal, own, from_left, from_right, *fields)


def finish_kernel(scal, z0, z1, noise, *rest):
    out = rest[-1]
    k = pl.program_id(0)

    @pl.when(k == 0)
    def _():
        out[...] = z0[...] + noise[...]

    @pl.when(k == 1)
    def _():
        out[...] = z1[...] + noise[...]


def finish_step(scal, z0, z1, noise, chunk, out=None):
    per = 4 // CHUNKS

    def place(k, i, scal):
        d = chunk * per + i
        half = jnp.where(k == 0, scal[1], 1 - scal[1])
        return (jnp.where(half == 0, d, 7 - d), 0)

    first = pl.BlockSpec((192, 384), lambda k, i, scal: (jnp.where(k == 0, i, per - 1), 0))
    second = pl.BlockSpec((192, 384), lambda k, i, scal: (jnp.where(k == 1, i, 0), 0))
    block = pl.BlockSpec((192, 384), place)
    extra = [] if out is None else [out]
    return pl.pallas_call(
        finish_kernel,
        grid_spec=pltpu.PrefetchScalarGridSpec(
            num_scalar_prefetch=1,
            grid=(2, per),
            in_specs=[first, second, block] + [pl.BlockSpec(memory_space=pl.ANY)] * len(extra),
            out_specs=block,
        ),
        out_shape=shape(1536, 384),
        input_output_aliases={} if out is None else {4: 0},
        compiler_params=params(12),
        name="finish_step",
    )(scal, z0, z1, noise, *extra)


def permutations(rows, cols):
    def joint(r, z, a, b):
        return r * cols + z * 4 + a * 2 + b

    split, boundary, back = [[], []], [[], []], [[], []]
    for k in range(2):
        for r in range(rows):
            for z in range(cols // 4):
                for lo in range(2):
                    for core in range(2):
                        me = joint(r, z, lo, core)
                        split[k].append((me, joint(r, z, core ^ k, lo)))
                        if core == k and r + 1 < rows:
                            boundary[k].append((me, joint(r + 1, z, 0, lo)))
                        if core != k and r > 0:
                            boundary[k].append((me, joint(r - 1, z, 1, lo)))
                        back[k].append((me, joint(r, z, core, lo ^ k)))
    rightward = []
    for z in range(cols // 4):
        for p in range(2):
            rightward.append((z * 4 + p * 2, z * 4 + p * 2 + 1))
            if z + 1 < cols // 4:
                rightward.append((z * 4 + p * 2 + 1, (z + 1) * 4 + p * 2))
    leftward = [(b, a) for a, b in rightward]
    return split, boundary, back, rightward, leftward


def shards(covariance, process_noise, depth_field, coriolis, drag_rate):
    fields = (depth_field, coriolis, drag_rate)
    rows, cols = lax.axis_size("row"), lax.axis_size("col")
    split, boundary, back, rightward, leftward = permutations(rows, cols)
    row, col = lax.axis_index("row"), lax.axis_index("col")
    z, second, core = col // 4, (col // 2) % 2, col % 2
    both = ("row", "col")

    scal = jnp.stack([row * 8, core]).astype(jnp.int32)
    s00, s01, s10, s11, b0, b1 = rows_step(scal, covariance, fields)
    m0 = lax.ppermute(b0, both, boundary[0])
    m1 = lax.ppermute(b1, both, boundary[1])
    pieces = [
        [lax.ppermute(s, both, split[k]) for k, s in enumerate(pair)] for pair in ((s00, s10), (s01, s11))
    ]
    rscal = jnp.stack([row * 8 + second * 4, second]).astype(jnp.int32)
    r0, r1 = rows_response(rscal, m0, m1, fields)

    cscal = jnp.stack([(z * 2 + core) * 4, second]).astype(jnp.int32)
    result = None
    fscal = jnp.stack([row, core]).astype(jnp.int32)
    for chunk, (s0, s1) in enumerate(pieces):
        own, left, right = columns_step(cscal, s0, s1, r0, r1, fields, chunk)
        from_left = lax.ppermute(right, "col", rightward)
        from_right = lax.ppermute(left, "col", leftward)
        z0, z1 = columns_response(cscal, own, from_left, from_right, fields)
        z0 = lax.ppermute(z0, both, back[0])
        z1 = lax.ppermute(z1, both, back[1])
        result = finish_step(fscal, z0, z1, process_noise, chunk, result)
    return result


def solution(mesh):
    return jax.shard_map(
        shards,
        mesh=mesh,
        in_specs=(P("row", "col"), P("row", "col"), P(), P(), P()),
        out_specs=P("row", "col"),
        check_vma=False,
    )
```

```python
import functools

import jax
import jax.numpy as jnp
from jax import lax
from jax.experimental import pallas as pl
from jax.experimental.pallas import tpu as pltpu
from jax.sharding import PartitionSpec as P

GX = 64
STEP = 0.9
SEG = 72
LANES = 128
CHUNKS = 2
D, F, R, B = 0, 1, 2, 3
MIB = 1024 * 1024


def at(row, comp):
    return (row * 3 + comp) * SEG + 8


def buffer_rows(rows):
    return rows * 3 * SEG + 8


def zero_gaps(ref, rows):
    for i in range(rows * 3 + 1):
        ref[pl.ds(i * SEG, 8), :] = jnp.zeros((8, LANES), jnp.float32)


def load_coefficients(dep_ref, cor_ref, drag_ref, first, count, coef_ref, slot_of=None, turn=None, only=None):
    shift = lax.rem(128 - first + 128, 128)
    lane = lax.broadcasted_iota(jnp.int32, (GX, LANES), 1)
    inside = jnp.where(lane < GX, 1.0, 0.0).astype(jnp.float32)

    def rolled(ref, scale):
        wide = jnp.concatenate([ref[...].T, jnp.zeros((GX, LANES - GX), jnp.float32)], axis=1)
        return pltpu.roll(wide * scale, shift, 1)

    tables = {
        D: rolled(dep_ref, -0.5 * STEP),
        F: rolled(cor_ref, STEP),
        R: rolled(drag_ref, STEP),
        B: pltpu.roll(inside * (-0.5 * STEP), shift, 1),
    }
    if turn is not None:
        tables[F] = tables[F] * turn
    for j in only or range(count):
        slot = j if slot_of is None else slot_of(j)
        for kind, table in tables.items():
            coef_ref[slot, kind] = jnp.broadcast_to(table[:, j : j + 1], (GX, LANES))


def total(terms):
    terms = [t for t in terms if t is not None]
    if not terms:
        return None
    acc = terms[0]
    for t in terms[1:]:
        acc = acc + t
    return acc


def tendency(src, have, row, base, coef, slot, ghost=False, want=(0, 1, 2), turn=1):
    def get(r, c, shift=0):
        return src[pl.ds(at(r + base, c) + shift, GX), :]

    def diff_x(c):
        return get(row, c, 1) - get(row, c, -1)

    def diff_y(c):
        above, below = (row + 1, c) in have, (row - 1, c) in have
        if above and below:
            return get(row + 1, c) - get(row - 1, c)
        if above:
            return get(row + 1, c)
        if below:
            return -get(row - 1, c)
        return None

    half = coef[slot, B] if ghost else jnp.float32(-0.5 * STEP)
    center = [get(row, c) if (row, c) in have else None for c in range(3)]
    out = {}
    if 0 in want:
        s = total([diff_x(1) if center[1] is not None else None, diff_y(2)])
        out[0] = None if s is None else coef[slot, D] * s
    if 1 in want:
        dx = half * diff_x(0) if center[0] is not None else None
        spin = None if center[2] is None else (turn * coef[slot, F] if turn != 1 else coef[slot, F]) * center[2]
        drag = None if center[1] is None else -(coef[slot, R] * center[1])
        out[1] = total([dx, spin, drag])
    if 2 in want:
        dy = diff_y(0)
        dy = None if dy is None else half * dy
        spin = None if center[1] is None else (-turn * coef[slot, F]) * center[1]
        drag = None if center[2] is None else -(coef[slot, R] * center[2])
        out[2] = total([dy, spin, drag])
    return out


def powers(bufs, rows, base, coef, finish):
    have = {(r, c) for r in range(rows) for c in range(3)}
    for j, reach in ((1, 1), (2, 2), (3, 1)):
        new = set()
        for r in range(-reach, rows + reach):
            ghost = r < 0 or r >= rows
            want = (0, 2) if ghost and j == 3 else (0, 1, 2)
            out = tendency(bufs[j - 1], have, r, base, coef, r + 2, ghost, want)
            for c, v in out.items():
                if v is not None:
                    bufs[j][pl.ds(at(r + base, c), GX), :] = v if j == 1 else v * (1.0 / j)
                    new.add((r, c))
        have = new
    for r in range(rows):
        out = tendency(bufs[3], have, r, base, coef, r + 2)
        for c in range(3):
            finish(r, c, out[c] * 0.25)


FACT = [1.0, 1.0, 2.0, 6.0, 24.0]


def response(message, bufs, base, coef, slot_of, finish, turn=1, powers_in=(0, 1, 2, 3)):
    heights = {j: message(j, 0) for j in powers_in}
    norths = {j: message(j, 1) for j in powers_in}

    def force(m):
        weights = {j: FACT[j] / FACT[j + 1 + m] for j in powers_in if j <= 3 - m}
        if not weights:
            return None, None
        fh = total([w * heights[j] for j, w in weights.items()])
        fn = total([w * norths[j] for j, w in weights.items()])
        return -(coef[slot_of(0), D] * fn), (0.5 * STEP) * fh

    have = set()
    src = None
    for step, m in enumerate((3, 2, 1, 0)):
        new = set()
        for d in range(step + 1):
            out = {0: None, 1: None, 2: None}
            if src is not None:
                out = tendency(src, have, d, base, coef, slot_of(d), turn=turn)
            if d == 0:
                fh, fn = force(m)
                out[0] = total([out[0], fh])
                out[2] = total([out[2], fn])
            for c, v in out.items():
                if m == 0:
                    finish(d, c, v)
                elif v is not None:
                    bufs[step % 2][pl.ds(at(d + base, c), GX), :] = v
                    new.add((d, c))
        have, src = new, bufs[step % 2]


def rows_kernel(x_ref, dep, cor, drag, s00, s01, s10, s11, e0, e1, b0, b1, coef, v0, v1, v2, v3, acc):
    rows, base = 8, 2

    @pl.when(pl.program_id(0) == 0)
    def _():
        load_coefficients(dep, cor, drag, lax.axis_index("row") * rows - 2, rows + 4, coef)
        for ref in (v0, v1, v2, v3):
            zero_gaps(ref, rows + 4)

    for r in range(rows):
        for c in range(3):
            v0[pl.ds(at(r + base, c), GX), :] = x_ref[pl.ds((r * 3 + c) * GX, GX), :]

    def finish(r, c, v4):
        half, d = (0, r) if r < 4 else (1, 7 - r)
        place = half * 4 + (d + 2) % 4
        i = at(r + base, c)
        v = v4 + v3[pl.ds(i, GX), :] + v2[pl.ds(i, GX), :] + v1[pl.ds(i, GX), :] + v0[pl.ds(i, GX), :]
        acc[pl.ds((place * 3 + c) * GX, GX), :] = v

    powers((v0, v1, v2, v3), rows, base, coef, finish)

    def put(e_ref, b_ref, row):
        for j, ref in enumerate((v0, v1, v2, v3)):
            for i, c in enumerate((0, 2)):
                to = e_ref if j < 2 else b_ref
                to[pl.ds((j % 2 * 2 + i) * GX, GX), :] = ref[pl.ds(at(row + base, c), GX), :]

    half, part = 768, 384
    core = lax.axis_index("col") % 2

    @pl.when(core == 0)
    def _():
        s00[...] = acc[pl.ds(0, part), :]
        s01[...] = acc[pl.ds(part, part), :]
        s10[...] = acc[pl.ds(half, part), :]
        s11[...] = acc[pl.ds(half + part, part), :]
        put(e0, b0, 7)
        put(e1, b1, 0)

    @pl.when(core == 1)
    def _():
        s10[...] = acc[pl.ds(0, part), :]
        s11[...] = acc[pl.ds(part, part), :]
        s00[...] = acc[pl.ds(half, part), :]
        s01[...] = acc[pl.ds(half + part, part), :]
        put(e1, b1, 7)
        put(e0, b0, 0)


def whole(ref_shape):
    return pl.BlockSpec(ref_shape, lambda i, *_: tuple(0 for _ in ref_shape))


def vmem(rows, cols=LANES):
    return pltpu.VMEM((rows, cols), jnp.float32)


def shape(rows, cols):
    return jax.ShapeDtypeStruct((rows, cols), jnp.float32)


def params(mib):
    return pltpu.CompilerParams(vmem_limit_bytes=mib * MIB)


def lane_block(rows):
    return pl.BlockSpec((rows, LANES), lambda i, *_: (0, i))


def rows_step(block, fields):
    table = whole((GX, GX))
    buf = vmem(buffer_rows(12))
    return pl.pallas_call(
        rows_kernel,
        grid_spec=pltpu.PrefetchScalarGridSpec(
            num_scalar_prefetch=0,
            grid=(3,),
            in_specs=[lane_block(1536), table, table, table],
            out_specs=[lane_block(384)] * 4 + [lane_block(256)] * 4,
            scratch_shapes=[pltpu.VMEM((12, 4, GX, LANES), jnp.float32), buf, buf, buf, buf, vmem(1536)],
        ),
        out_shape=[shape(384, 384)] * 4 + [shape(256, 384)] * 4,
        compiler_params=params(58),
        name="rows_step",
    )(block, *fields)


def rows_response_kernel(powers_in, scal, m0, m1, *refs):
    late = powers_in[0] > 0
    before, (dep, cor, drag), refs = refs[: 3 * late], refs[3 * late : 3 * late + 3], refs[3 * late + 3 :]
    outs, (coef, t0, t1) = refs[:-3], refs[-3:]
    half = scal[1]
    turn = 1.0 - 2.0 * half.astype(jnp.float32)

    @pl.when(pl.program_id(0) == 0)
    def _():
        load_coefficients(dep, cor, drag, scal[0], 4, coef, lambda j: jnp.where(half == 0, j, 3 - j), turn)
        for ref in (t0, t1):
            zero_gaps(ref, 4)

    for k, m_ref in enumerate((m0, m1)):

        def message(j, i, m_ref=m_ref):
            v = m_ref[pl.ds(((j % 2) * 2 + i) * GX, GX), :]
            return v * turn if i == 1 else v

        def finish(d, c, v, k=k):
            if late and d > 1:
                return
            i = pl.ds((d % 2 * 3 + c) * GX, GX)
            v = jnp.zeros((GX, LANES), jnp.float32) if v is None else v
            v = v * turn if c == 2 else v
            if late:
                outs[k][i, :] = before[k][i, :] + v
            else:
                outs[k + 2 * (d < 2)][i, :] = v

        response(message, (t0, t1), 0, coef, lambda d: d, finish, powers_in=powers_in)


def rows_response(scal, messages, fields, powers_in, before=(), after=()):
    table = whole((GX, GX))
    buf = vmem(buffer_rows(4))
    count = 2 if before else 4
    return pl.pallas_call(
        functools.partial(rows_response_kernel, powers_in),
        grid_spec=pltpu.PrefetchScalarGridSpec(
            num_scalar_prefetch=1,
            grid=(3,),
            in_specs=[lane_block(256)] * 2
            + [lane_block(384)] * len(before)
            + [pl.BlockSpec(memory_space=pl.ANY)] * len(after)
            + [table] * 3,
            out_specs=[lane_block(384)] * count,
            scratch_shapes=[pltpu.VMEM((4, 4, GX, LANES), jnp.float32), buf, buf],
        ),
        out_shape=[shape(384, 384)] * count,
        compiler_params=params(16),
        name="rows_response",
    )(scal, *messages, *before, *after, *fields)


def columns_kernel(scal, s0, s1, r0, r1, dep, cor, drag, out, inner, outer, coef, v0, v1, v2, v3):
    rows, base = 4, 2
    half = scal[1]

    @pl.when(pl.program_id(0) == 0)
    def _():
        load_coefficients(dep, cor, drag, scal[0] - 2, rows + 4, coef)
        for ref in (v0, v1, v2, v3):
            zero_gaps(ref, rows + 4)

    for k, (s_ref, r_ref) in enumerate(((s0, r0), (s1, r1))):
        core = half if k == 0 else 1 - half
        start = pl.multiple_of(core * (2 * 3 * SEG), 8)
        for t in range(3):
            piece = (s_ref[:, t * LANES : (t + 1) * LANES] + r_ref[:, t * LANES : (t + 1) * LANES]).T
            for i in range(2):
                seg = t * 2 + i
                place = pl.multiple_of(start + (base * 3 + seg) * SEG + 8, 8)
                v0[pl.ds(place, GX), :] = piece[i * GX : (i + 1) * GX, :]

    def finish(r, c, v4):
        i = at(r + base, c)
        v = v4 + v3[pl.ds(i, GX), :] + v2[pl.ds(i, GX), :] + v1[pl.ds(i, GX), :] + v0[pl.ds(i, GX), :]
        out[pl.ds((r * 3 + c) * GX, GX), :] = v

    powers((v0, v1, v2, v3), rows, base, coef, finish)

    def put(to, row):
        for j, ref in enumerate((v0, v1, v2, v3)):
            for i, c in enumerate((0, 2)):
                to[pl.ds((j * 2 + i) * GX, GX), :] = ref[pl.ds(at(row + base, c), GX), :]

    @pl.when(scal[2] == 0)
    def _():
        put(inner, rows - 1)
        put(outer, 0)

    @pl.when(scal[2] == 1)
    def _():
        put(inner, 0)
        put(outer, rows - 1)


def columns_step(scal, s0, s1, r0, r1, fields):
    table = whole((GX, GX))
    part = 768 // CHUNKS
    tiles = part // LANES
    buf = vmem(buffer_rows(8))
    return pl.pallas_call(
        columns_kernel,
        grid_spec=pltpu.PrefetchScalarGridSpec(
            num_scalar_prefetch=1,
            grid=(tiles,),
            in_specs=[pl.BlockSpec((LANES, 384), lambda i, *_: (i, 0))] * 4 + [table] * 3,
            out_specs=[lane_block(768), lane_block(512), lane_block(512)],
            scratch_shapes=[pltpu.VMEM((8, 4, GX, LANES), jnp.float32), buf, buf, buf, buf],
        ),
        out_shape=[shape(768, part), shape(512, part), shape(512, part)],
        compiler_params=params(24),
        name="columns_step",
    )(scal, s0, s1, r0, r1, *fields)


def columns_response_kernel(scal, own, inner, outer, dep, cor, drag, z0, z1, coef, t0, t1, acc):
    half = scal[1]

    @pl.when(pl.program_id(0) == 0)
    def _():
        load_coefficients(dep, cor, drag, scal[0], 4, coef)
        for ref in (t0, t1):
            zero_gaps(ref, 4)

    def message_left(j, i):
        place = pl.ds((j * 2 + i) * GX, GX)
        return jnp.where(scal[2] == 0, outer[place, :], inner[place, :])

    def finish_left(d, c, v):
        i = pl.ds((d * 3 + c) * GX, GX)
        acc[i, :] = own[i, :] if v is None else own[i, :] + v

    response(message_left, (t0, t1), 0, coef, lambda d: d, finish_left)

    def message_right(j, i):
        place = pl.ds((j * 2 + i) * GX, GX)
        v = jnp.where(scal[2] == 0, inner[place, :], outer[place, :])
        return -v if i == 1 else v

    def finish_right(d, c, v):
        i = pl.ds(((3 - d) * 3 + c) * GX, GX)
        if v is not None:
            acc[i, :] = acc[i, :] + (-v if c == 2 else v)

    response(message_right, (t0, t1), 0, coef, lambda d: 3 - d, finish_right, turn=-1)
    for k, z_ref in enumerate((z0, z1)):
        core = half if k == 0 else 1 - half
        for t in range(3):
            place = pl.multiple_of(core * 384 + t * LANES, LANES)
            z_ref[:, t * LANES : (t + 1) * LANES] = acc[pl.ds(place, LANES), :].T


def columns_response(scal, own, inner, outer, fields):
    table = whole((GX, GX))
    part = 768 // CHUNKS
    buf = vmem(buffer_rows(4))
    return pl.pallas_call(
        columns_response_kernel,
        grid_spec=pltpu.PrefetchScalarGridSpec(
            num_scalar_prefetch=1,
            grid=(part // LANES,),
            in_specs=[lane_block(768), lane_block(512), lane_block(512)] + [table] * 3,
            out_specs=[pl.BlockSpec((LANES, 384), lambda i, *_: (i, 0))] * 2,
            scratch_shapes=[pltpu.VMEM((4, 4, GX, LANES), jnp.float32), buf, buf, vmem(768)],
        ),
        out_shape=[shape(part, 384)] * 2,
        compiler_params=params(16),
        name="columns_response",
    )(scal, own, inner, outer, *fields)


def finish_kernel(scal, z0, z1, noise, *rest):
    out = rest[-1]
    k = pl.program_id(0)
    half = jnp.where(k == 0, scal[1], 1 - scal[1])

    def put(z, flip):
        for d in range(2):
            place = pl.ds((1 - d if flip else d) * 192, 192)
            out[place, :] = z[pl.ds(d * 192, 192), :] + noise[place, :]

    for i, z in enumerate((z0, z1)):
        for flip in (False, True):
            pl.when(jnp.logical_and(k == i, half == int(flip)))(functools.partial(put, z, flip))


def finish_step(scal, z0, z1, noise, near, out=None):
    def place(k, scal):
        half = jnp.where(k == 0, scal[1], 1 - scal[1])
        return (jnp.where(half == 0, 0, 3) if near else 1 + half, 0)

    full = pl.BlockSpec((384, 384), lambda k, scal: (0, 0))
    block = pl.BlockSpec((384, 384), place)
    extra = [] if out is None else [out]
    return pl.pallas_call(
        finish_kernel,
        grid_spec=pltpu.PrefetchScalarGridSpec(
            num_scalar_prefetch=1,
            grid=(2,),
            in_specs=[full, full, block] + [pl.BlockSpec(memory_space=pl.ANY)] * len(extra),
            out_specs=block,
        ),
        out_shape=shape(1536, 384),
        input_output_aliases={} if out is None else {4: 0},
        compiler_params=params(12),
        name="finish_step",
    )(scal, z0, z1, noise, *extra)


def permutations(rows, cols):
    def joint(r, z, a, b):
        return r * cols + z * 4 + a * 2 + b

    split, boundary, back = [[], []], [[], []], [[], []]
    for k in range(2):
        for r in range(rows):
            for z in range(cols // 4):
                for lo in range(2):
                    for core in range(2):
                        me = joint(r, z, lo, core)
                        split[k].append((me, joint(r, z, core ^ k, lo)))
                        if core == k and r + 1 < rows:
                            boundary[k].append((me, joint(r + 1, z, 0, lo)))
                        if core != k and r > 0:
                            boundary[k].append((me, joint(r - 1, z, 1, lo)))
                        back[k].append((me, joint(r, z, core, lo ^ k)))
    inner = [(i, i ^ 1) for i in range(cols)]
    outer = []
    for z in range(cols // 4 - 1):
        for p in range(2):
            a, b = z * 4 + p * 2 + 1, (z + 1) * 4 + p * 2
            outer += [(a, b), (b, a)]
    return split, boundary, back, inner, outer


def shards(covariance, process_noise, depth_field, coriolis, drag_rate):
    fields = (depth_field, coriolis, drag_rate)
    rows, cols = lax.axis_size("row"), lax.axis_size("col")
    split, boundary, back, inner, outer = permutations(rows, cols)
    row, col = lax.axis_index("row"), lax.axis_index("col")
    z, second, core = col // 4, (col // 2) % 2, col % 2
    both = ("row", "col")

    def send(pair, pairs):
        return [lax.ppermute(v, both, pairs[k]) for k, v in enumerate(pair)]

    s00, s01, s10, s11, e0, e1, b0, b1 = rows_step(covariance, fields)
    early = send((e0, e1), boundary)
    far = send((s00, s10), split)
    b0, b1, *early = lax.optimization_barrier((b0, b1, *early))
    late = send((b0, b1), boundary)
    near = send((s01, s11), split)
    rscal = jnp.stack([row * 8 + second * 4, second]).astype(jnp.int32)
    cscal = jnp.stack([(z * 2 + core) * 4, second, core]).astype(jnp.int32)
    fscal = jnp.stack([row, core]).astype(jnp.int32)
    r02, r12, r00, r10 = rows_response(rscal, early, fields, (0, 1))
    result = None
    for chunk, halves, moved in ((0, far, (r02, r12)), (1, near, None)):
        if chunk == 1:
            moved = rows_response(rscal, late, fields, (2, 3), (r00, r10), (own,))
        own, inside, outside = columns_step(cscal, *halves, *moved, fields)
        outside = lax.ppermute(outside, "col", outer)
        inside = lax.ppermute(inside, "col", inner)
        ready = send(columns_response(cscal, own, inside, outside, fields), back)
        result = finish_step(fscal, *ready, process_noise, chunk == 1, result)
    return result


def solution(mesh):
    return jax.shard_map(
        shards,
        mesh=mesh,
        in_specs=(P("row", "col"), P("row", "col"), P(), P(), P()),
        out_specs=P("row", "col"),
        check_vma=False,
    )
```

```python
import functools

import jax
import jax.numpy as jnp
from jax import lax
from jax.experimental import pallas as pl
from jax.experimental.pallas import tpu as pltpu
from jax.sharding import PartitionSpec as P

GX = 64
STEP = 0.9
SEG = 72
LANES = 128
CHUNKS = 2
D, F, R, B = 0, 1, 2, 3
MIB = 1024 * 1024


def at(row, comp):
    return (row * 3 + comp) * SEG + 8


def buffer_rows(rows):
    return rows * 3 * SEG + 8


def zero_gaps(ref, rows):
    for i in range(rows * 3 + 1):
        ref[pl.ds(i * SEG, 8), :] = jnp.zeros((8, LANES), jnp.float32)


def load_coefficients(dep_ref, cor_ref, drag_ref, first, count, coef_ref, slot_of=None, turn=None, only=None):
    shift = lax.rem(128 - first + 128, 128)
    lane = lax.broadcasted_iota(jnp.int32, (GX, LANES), 1)
    inside = jnp.where(lane < GX, 1.0, 0.0).astype(jnp.float32)

    def rolled(ref, scale):
        wide = jnp.concatenate([ref[...].T, jnp.zeros((GX, LANES - GX), jnp.float32)], axis=1)
        return pltpu.roll(wide * scale, shift, 1)

    tables = {
        D: rolled(dep_ref, -0.5 * STEP),
        F: rolled(cor_ref, STEP),
        R: rolled(drag_ref, STEP),
        B: pltpu.roll(inside * (-0.5 * STEP), shift, 1),
    }
    if turn is not None:
        tables[F] = tables[F] * turn
    for j in only or range(count):
        slot = j if slot_of is None else slot_of(j)
        for kind, table in tables.items():
            coef_ref[slot, kind] = jnp.broadcast_to(table[:, j : j + 1], (GX, LANES))


def total(terms):
    terms = [t for t in terms if t is not None]
    if not terms:
        return None
    acc = terms[0]
    for t in terms[1:]:
        acc = acc + t
    return acc


def tendency(src, have, row, base, coef, slot, ghost=False, want=(0, 1, 2), turn=1):
    def get(r, c, shift=0):
        return src[pl.ds(at(r + base, c) + shift, GX), :]

    def diff_x(c):
        return get(row, c, 1) - get(row, c, -1)

    def diff_y(c):
        above, below = (row + 1, c) in have, (row - 1, c) in have
        if above and below:
            return get(row + 1, c) - get(row - 1, c)
        if above:
            return get(row + 1, c)
        if below:
            return -get(row - 1, c)
        return None

    half = coef[slot, B] if ghost else jnp.float32(-0.5 * STEP)
    center = [get(row, c) if (row, c) in have else None for c in range(3)]
    out = {}
    if 0 in want:
        s = total([diff_x(1) if center[1] is not None else None, diff_y(2)])
        out[0] = None if s is None else coef[slot, D] * s
    if 1 in want:
        dx = half * diff_x(0) if center[0] is not None else None
        spin = None if center[2] is None else (turn * coef[slot, F] if turn != 1 else coef[slot, F]) * center[2]
        drag = None if center[1] is None else -(coef[slot, R] * center[1])
        out[1] = total([dx, spin, drag])
    if 2 in want:
        dy = diff_y(0)
        dy = None if dy is None else half * dy
        spin = None if center[1] is None else (-turn * coef[slot, F]) * center[1]
        drag = None if center[2] is None else -(coef[slot, R] * center[2])
        out[2] = total([dy, spin, drag])
    return out


def powers(bufs, rows, base, coef, finish):
    have = {(r, c) for r in range(rows) for c in range(3)}
    for j, reach in ((1, 1), (2, 2), (3, 1)):
        new = set()
        for r in range(-reach, rows + reach):
            ghost = r < 0 or r >= rows
            want = (0, 2) if ghost and j == 3 else (0, 1, 2)
            out = tendency(bufs[j - 1], have, r, base, coef, r + 2, ghost, want)
            for c, v in out.items():
                if v is not None:
                    bufs[j][pl.ds(at(r + base, c), GX), :] = v if j == 1 else v * (1.0 / j)
                    new.add((r, c))
        have = new
    for r in range(rows):
        out = tendency(bufs[3], have, r, base, coef, r + 2)
        for c in range(3):
            finish(r, c, out[c] * 0.25)


FACT = [1.0, 1.0, 2.0, 6.0, 24.0]


def response(message, bufs, base, coef, slot_of, finish, turn=1, powers_in=(0, 1, 2, 3)):
    heights = {j: message(j, 0) for j in powers_in}
    norths = {j: message(j, 1) for j in powers_in}

    def force(m):
        weights = {j: FACT[j] / FACT[j + 1 + m] for j in powers_in if j <= 3 - m}
        if not weights:
            return None, None
        fh = total([w * heights[j] for j, w in weights.items()])
        fn = total([w * norths[j] for j, w in weights.items()])
        return -(coef[slot_of(0), D] * fn), (0.5 * STEP) * fh

    have = set()
    src = None
    for step, m in enumerate((3, 2, 1, 0)):
        new = set()
        for d in range(step + 1):
            out = {0: None, 1: None, 2: None}
            if src is not None:
                out = tendency(src, have, d, base, coef, slot_of(d), turn=turn)
            if d == 0:
                fh, fn = force(m)
                out[0] = total([out[0], fh])
                out[2] = total([out[2], fn])
            for c, v in out.items():
                if m == 0:
                    finish(d, c, v)
                elif v is not None:
                    bufs[step % 2][pl.ds(at(d + base, c), GX), :] = v
                    new.add((d, c))
        have, src = new, bufs[step % 2]


EDGE_ROWS = (0, 1, 2, 5, 6, 7)


def edge_kernel(*refs):
    rows, (dep, cor, drag, e0, e1, coef, u0, u1) = refs[:6], refs[6:]
    base = 1
    load_coefficients(dep, cor, drag, lax.axis_index("row") * 8 - base, 10, coef, only=(0, 1, 2, 7, 8, 9))
    for ref in (u0, u1):
        zero_gaps(ref, 10)
    core = lax.axis_index("col") % 2
    have = {(r, c) for r in EDGE_ROWS for c in range(3)}

    @pl.loop(0, 3)
    def _(tile):
        lanes = pl.ds(pl.multiple_of(tile * LANES, LANES), LANES)
        for r, ref in zip(EDGE_ROWS, rows):
            for c in range(3):
                u0[pl.ds(at(r + base, c), GX), :] = ref[pl.ds(c * GX, GX), lanes]
        new = set()
        for r in (-1, 0, 1, 6, 7, 8):
            out = tendency(u0, have, r, base, coef, r + base, ghost=r in (-1, 8))
            for c, v in out.items():
                if v is not None:
                    u1[pl.ds(at(r + base, c), GX), :] = v
                    new.add((r, c))

        def put(to, row):
            out = tendency(u1, new, row, base, coef, row + base, want=(0, 2))
            for i, c in enumerate((0, 2)):
                place = pl.multiple_of(tile * 384 + i * GX, GX)
                to[pl.ds(place, GX), :] = u0[pl.ds(at(row + base, c), GX), :]
                to[pl.ds(place + 2 * GX, GX), :] = u1[pl.ds(at(row + base, c), GX), :]
                to[pl.ds(place + 4 * GX, GX), :] = out[c] * 0.5

        @pl.when(core == 0)
        def _():
            put(e0, 7)
            put(e1, 0)

        @pl.when(core == 1)
        def _():
            put(e1, 7)
            put(e0, 0)


def edge_step(block, fields):
    table = whole((GX, GX))
    buf = vmem(buffer_rows(10))
    return pl.pallas_call(
        edge_kernel,
        grid=(1,),
        in_specs=[pl.BlockSpec((192, 384), lambda i, r=r: (r, 0)) for r in EDGE_ROWS] + [table] * 3,
        out_specs=[whole((1152, LANES))] * 2,
        scratch_shapes=[pltpu.VMEM((10, 4, GX, LANES), jnp.float32), buf, buf],
        out_shape=[shape(1152, LANES)] * 2,
        compiler_params=params(58),
        name="edge_step",
    )(*[block] * 6, *fields)


def rows_kernel(x_ref, after, dep, cor, drag, s00, s01, s10, s11, b0, b1, coef, v0, v1, v2, v3, acc):
    rows, base = 8, 2

    @pl.when(pl.program_id(0) == 0)
    def _():
        load_coefficients(dep, cor, drag, lax.axis_index("row") * rows - 2, rows + 4, coef)
        for ref in (v0, v1, v2, v3):
            zero_gaps(ref, rows + 4)

    for r in range(rows):
        for c in range(3):
            v0[pl.ds(at(r + base, c), GX), :] = x_ref[pl.ds((r * 3 + c) * GX, GX), :]

    def finish(r, c, v4):
        half, d = (0, r) if r < 4 else (1, 7 - r)
        place = half * 4 + (d + 2) % 4
        i = at(r + base, c)
        v = v4 + v3[pl.ds(i, GX), :] + v2[pl.ds(i, GX), :] + v1[pl.ds(i, GX), :] + v0[pl.ds(i, GX), :]
        acc[pl.ds((place * 3 + c) * GX, GX), :] = v

    powers((v0, v1, v2, v3), rows, base, coef, finish)

    def put(to, row):
        for i, c in enumerate((0, 2)):
            to[pl.ds(i * GX, GX), :] = v3[pl.ds(at(row + base, c), GX), :]

    half, part = 768, 384
    core = lax.axis_index("col") % 2

    @pl.when(core == 0)
    def _():
        s00[...] = acc[pl.ds(0, part), :]
        s01[...] = acc[pl.ds(part, part), :]
        s10[...] = acc[pl.ds(half, part), :]
        s11[...] = acc[pl.ds(half + part, part), :]
        put(b0, 7)
        put(b1, 0)

    @pl.when(core == 1)
    def _():
        s10[...] = acc[pl.ds(0, part), :]
        s11[...] = acc[pl.ds(part, part), :]
        s00[...] = acc[pl.ds(half, part), :]
        s01[...] = acc[pl.ds(half + part, part), :]
        put(b1, 7)
        put(b0, 0)


def whole(ref_shape):
    return pl.BlockSpec(ref_shape, lambda i, *_: tuple(0 for _ in ref_shape))


def vmem(rows, cols=LANES):
    return pltpu.VMEM((rows, cols), jnp.float32)


def shape(rows, cols):
    return jax.ShapeDtypeStruct((rows, cols), jnp.float32)


def params(mib):
    return pltpu.CompilerParams(vmem_limit_bytes=mib * MIB)


def lane_block(rows):
    return pl.BlockSpec((rows, LANES), lambda i, *_: (0, i))


def stacked(rows):
    return pl.BlockSpec((rows, LANES), lambda i, *_: (i, 0))


def rows_step(block, after, fields):
    table = whole((GX, GX))
    buf = vmem(buffer_rows(12))
    return pl.pallas_call(
        rows_kernel,
        grid_spec=pltpu.PrefetchScalarGridSpec(
            num_scalar_prefetch=0,
            grid=(3,),
            in_specs=[lane_block(1536), pl.BlockSpec(memory_space=pl.ANY), table, table, table],
            out_specs=[lane_block(384)] * 4 + [lane_block(128)] * 2,
            scratch_shapes=[pltpu.VMEM((12, 4, GX, LANES), jnp.float32), buf, buf, buf, buf, vmem(1536)],
        ),
        out_shape=[shape(384, 384)] * 4 + [shape(128, 384)] * 2,
        compiler_params=params(58),
        name="rows_step",
    )(block, after, *fields)


def rows_response_kernel(scal, m0, m1, dep, cor, drag, *refs):
    outs, (coef, t0, t1) = refs[:-3], refs[-3:]
    half = scal[1]
    turn = 1.0 - 2.0 * half.astype(jnp.float32)

    @pl.when(pl.program_id(0) == 0)
    def _():
        load_coefficients(dep, cor, drag, scal[0], 4, coef, lambda j: jnp.where(half == 0, j, 3 - j), turn)
        for ref in (t0, t1):
            zero_gaps(ref, 4)

    for k, m_ref in enumerate((m0, m1)):

        def message(j, i, m_ref=m_ref):
            v = m_ref[pl.ds((j * 2 + i) * GX, GX), :]
            return v * turn if i == 1 else v

        def finish(d, c, v, k=k):
            v = jnp.zeros((GX, LANES), jnp.float32) if v is None else v
            outs[k + 2 * (d < 2)][pl.ds((d % 2 * 3 + c) * GX, GX), :] = v * turn if c == 2 else v

        response(message, (t0, t1), 0, coef, lambda d: d, finish, powers_in=(0, 1, 2))


def rows_response(scal, messages, fields):
    table = whole((GX, GX))
    buf = vmem(buffer_rows(4))
    return pl.pallas_call(
        rows_response_kernel,
        grid_spec=pltpu.PrefetchScalarGridSpec(
            num_scalar_prefetch=1,
            grid=(3,),
            in_specs=[stacked(384)] * 2 + [table] * 3,
            out_specs=[lane_block(384)] * 4,
            scratch_shapes=[pltpu.VMEM((4, 4, GX, LANES), jnp.float32), buf, buf],
        ),
        out_shape=[shape(384, 384)] * 4,
        compiler_params=params(16),
        name="rows_response",
    )(scal, *messages, *fields)


def columns_kernel(scal, s0, s1, r0, r1, *refs):
    late, (dep, cor, drag, out, inner, outer, coef, v0, v1, v2, v3, near, extra) = refs[:-13], refs[-13:]
    rows, base = 4, 2
    half = scal[1]

    @pl.when(pl.program_id(0) == 0)
    def _():
        load_coefficients(dep, cor, drag, scal[0] - 2, rows + 4, coef)
        for ref in (v0, v1, v2, v3):
            zero_gaps(ref, rows + 4)

    if late:
        turn = 1.0 - 2.0 * half.astype(jnp.float32)

        @pl.when(pl.program_id(0) == 0)
        def _():
            load_coefficients(dep, cor, drag, scal[3], 4, near, lambda j: jnp.where(half == 0, j, 3 - j))
            for k in range(2):
                for t in range(3):
                    lanes = pl.ds(t * LANES, LANES)
                    extra[pl.ds(k * GX, GX), lanes] = near[0, D] * (late[k][pl.ds(GX, GX), lanes] * (-0.25 * turn))

        @pl.when(pl.program_id(0) == 1)
        def _():
            for k in range(2):
                extra[pl.ds(k * GX, GX), :] = late[k][pl.ds(0, GX), :] * (0.125 * STEP * turn)

        @pl.when(pl.program_id(0) == 2)
        def _():
            extra[...] = jnp.zeros_like(extra)

    for k, (s_ref, r_ref) in enumerate(((s0, r0), (s1, r1))):
        core = half if k == 0 else 1 - half
        start = pl.multiple_of(core * (2 * 3 * SEG), 8)
        for t in range(3):
            lanes = slice(t * LANES, (t + 1) * LANES)
            piece = s_ref[:, lanes] + r_ref[:, lanes]
            if late:
                more = extra[pl.ds(k * GX, GX), lanes]
                piece = jnp.concatenate([piece[:GX] + more, piece[GX:]], axis=0)
            piece = piece.T
            for i in range(2):
                seg = t * 2 + i
                place = pl.multiple_of(start + (base * 3 + seg) * SEG + 8, 8)
                v0[pl.ds(place, GX), :] = piece[i * GX : (i + 1) * GX, :]

    def finish(r, c, v4):
        i = at(r + base, c)
        v = v4 + v3[pl.ds(i, GX), :] + v2[pl.ds(i, GX), :] + v1[pl.ds(i, GX), :] + v0[pl.ds(i, GX), :]
        out[pl.ds((r * 3 + c) * GX, GX), :] = v

    powers((v0, v1, v2, v3), rows, base, coef, finish)

    def put(to, row):
        for j, ref in enumerate((v0, v1, v2, v3)):
            for i, c in enumerate((0, 2)):
                to[pl.ds((j * 2 + i) * GX, GX), :] = ref[pl.ds(at(row + base, c), GX), :]

    @pl.when(scal[2] == 0)
    def _():
        put(inner, rows - 1)
        put(outer, 0)

    @pl.when(scal[2] == 1)
    def _():
        put(inner, 0)
        put(outer, rows - 1)


def columns_step(scal, s0, s1, r0, r1, late, fields):
    table = whole((GX, GX))
    part = 768 // CHUNKS
    buf = vmem(buffer_rows(8))
    return pl.pallas_call(
        columns_kernel,
        grid_spec=pltpu.PrefetchScalarGridSpec(
            num_scalar_prefetch=1,
            grid=(part // LANES,),
            in_specs=[pl.BlockSpec((LANES, 384), lambda i, *_: (i, 0))] * 4
            + [whole((128, 384))] * len(late)
            + [table] * 3,
            out_specs=[stacked(768), stacked(512), stacked(512)],
            scratch_shapes=[
                pltpu.VMEM((8, 4, GX, LANES), jnp.float32),
                *[buf] * 4,
                pltpu.VMEM((4, 4, GX, LANES), jnp.float32),
                vmem(2 * GX, 384),
            ],
        ),
        out_shape=[shape(part * 6, LANES), shape(part * 4, LANES), shape(part * 4, LANES)],
        compiler_params=params(24),
        name="columns_step",
    )(scal, s0, s1, r0, r1, *late, *fields)


def columns_response_kernel(scal, own, inner, outer, dep, cor, drag, z0, z1, coef, t0, t1, acc):
    half = scal[1]

    @pl.when(pl.program_id(0) == 0)
    def _():
        load_coefficients(dep, cor, drag, scal[0], 4, coef)
        for ref in (t0, t1):
            zero_gaps(ref, 4)

    def message_left(j, i):
        place = pl.ds((j * 2 + i) * GX, GX)
        return jnp.where(scal[2] == 0, outer[place, :], inner[place, :])

    def finish_left(d, c, v):
        i = pl.ds((d * 3 + c) * GX, GX)
        acc[i, :] = own[i, :] if v is None else own[i, :] + v

    response(message_left, (t0, t1), 0, coef, lambda d: d, finish_left)

    def message_right(j, i):
        place = pl.ds((j * 2 + i) * GX, GX)
        v = jnp.where(scal[2] == 0, inner[place, :], outer[place, :])
        return -v if i == 1 else v

    def finish_right(d, c, v):
        i = pl.ds(((3 - d) * 3 + c) * GX, GX)
        if v is not None:
            acc[i, :] = acc[i, :] + (-v if c == 2 else v)

    response(message_right, (t0, t1), 0, coef, lambda d: 3 - d, finish_right, turn=-1)
    for k, z_ref in enumerate((z0, z1)):
        core = half if k == 0 else 1 - half
        for t in range(3):
            place = pl.multiple_of(core * 384 + t * LANES, LANES)
            z_ref[:, t * LANES : (t + 1) * LANES] = acc[pl.ds(place, LANES), :].T


def columns_response(scal, own, inner, outer, fields):
    table = whole((GX, GX))
    part = 768 // CHUNKS
    buf = vmem(buffer_rows(4))
    return pl.pallas_call(
        columns_response_kernel,
        grid_spec=pltpu.PrefetchScalarGridSpec(
            num_scalar_prefetch=1,
            grid=(part // LANES,),
            in_specs=[stacked(768), stacked(512), stacked(512)] + [table] * 3,
            out_specs=[pl.BlockSpec((LANES, 384), lambda i, *_: (i, 0))] * 2,
            scratch_shapes=[pltpu.VMEM((4, 4, GX, LANES), jnp.float32), buf, buf, vmem(768)],
        ),
        out_shape=[shape(part, 384)] * 2,
        compiler_params=params(16),
        name="columns_response",
    )(scal, own, inner, outer, *fields)


def finish_kernel(scal, z0, z1, noise, *rest):
    out = rest[-1]
    k = pl.program_id(0)
    half = jnp.where(k == 0, scal[1], 1 - scal[1])

    def put(z, flip):
        for d in range(2):
            place = pl.ds((1 - d if flip else d) * 192, 192)
            out[place, :] = z[pl.ds(d * 192, 192), :] + noise[place, :]

    for i, z in enumerate((z0, z1)):
        for flip in (False, True):
            pl.when(jnp.logical_and(k == i, half == int(flip)))(functools.partial(put, z, flip))


def finish_step(scal, z0, z1, noise, near, out=None):
    def place(k, scal):
        half = jnp.where(k == 0, scal[1], 1 - scal[1])
        return (jnp.where(half == 0, 0, 3) if near else 1 + half, 0)

    full = pl.BlockSpec((384, 384), lambda k, scal: (0, 0))
    block = pl.BlockSpec((384, 384), place)
    extra = [] if out is None else [out]
    return pl.pallas_call(
        finish_kernel,
        grid_spec=pltpu.PrefetchScalarGridSpec(
            num_scalar_prefetch=1,
            grid=(2,),
            in_specs=[full, full, block] + [pl.BlockSpec(memory_space=pl.ANY)] * len(extra),
            out_specs=block,
        ),
        out_shape=shape(1536, 384),
        input_output_aliases={} if out is None else {4: 0},
        compiler_params=params(12),
        name="finish_step",
    )(scal, z0, z1, noise, *extra)


def permutations(rows, cols):
    def joint(r, z, a, b):
        return r * cols + z * 4 + a * 2 + b

    split, boundary, back = [[], []], [[], []], [[], []]
    for k in range(2):
        for r in range(rows):
            for z in range(cols // 4):
                for lo in range(2):
                    for core in range(2):
                        me = joint(r, z, lo, core)
                        split[k].append((me, joint(r, z, core ^ k, lo)))
                        if core == k and r + 1 < rows:
                            boundary[k].append((me, joint(r + 1, z, 0, lo)))
                        if core != k and r > 0:
                            boundary[k].append((me, joint(r - 1, z, 1, lo)))
                        back[k].append((me, joint(r, z, core, lo ^ k)))
    inner = [(i, i ^ 1) for i in range(cols)]
    outer = []
    for z in range(cols // 4 - 1):
        for p in range(2):
            a, b = z * 4 + p * 2 + 1, (z + 1) * 4 + p * 2
            outer += [(a, b), (b, a)]
    return split, boundary, back, inner, outer


def shards(covariance, process_noise, depth_field, coriolis, drag_rate):
    fields = (depth_field, coriolis, drag_rate)
    rows, cols = lax.axis_size("row"), lax.axis_size("col")
    split, boundary, back, inner, outer = permutations(rows, cols)
    row, col = lax.axis_index("row"), lax.axis_index("col")
    z, second, core = col // 4, (col // 2) % 2, col % 2
    both = ("row", "col")

    def send(pair, pairs):
        return [lax.ppermute(v, both, pairs[k]) for k, v in enumerate(pair)]

    edges = edge_step(covariance, fields)
    early = send(edges, boundary)
    s00, s01, s10, s11, b0, b1 = rows_step(covariance, edges[0], fields)
    far = send((s00, s10), split)
    late = send((b0, b1), boundary)
    near = send((s01, s11), split)
    rscal = jnp.stack([row * 8 + second * 4, second]).astype(jnp.int32)
    cscal = jnp.stack([(z * 2 + core) * 4, second, core, row * 8 + second * 4]).astype(jnp.int32)
    fscal = jnp.stack([row, core]).astype(jnp.int32)
    r02, r12, r00, r10 = rows_response(rscal, early, fields)
    result = None
    for chunk, halves, moved, rest in ((0, far, (r02, r12), ()), (1, near, (r00, r10), late)):
        own, inside, outside = columns_step(cscal, *halves, *moved, rest, fields)
        outside = lax.ppermute(outside, "col", outer)
        inside = lax.ppermute(inside, "col", inner)
        ready = send(columns_response(cscal, own, inside, outside, fields), back)
        result = finish_step(fscal, *ready, process_noise, chunk == 1, result)
    return result


def solution(mesh):
    return jax.shard_map(
        shards,
        mesh=mesh,
        in_specs=(P("row", "col"), P("row", "col"), P(), P(), P()),
        out_specs=P("row", "col"),
        check_vma=False,
    )
```

```python
import functools

import jax
import jax.numpy as jnp
from jax import lax
from jax.experimental import pallas as pl
from jax.experimental.pallas import tpu as pltpu
from jax.sharding import PartitionSpec as P

GX = 64
STEP = 0.9
SEG = 72
LANES = 128
CHUNKS = 2
D, F, R, B = 0, 1, 2, 3
MIB = 1024 * 1024


def at(row, comp):
    return (row * 3 + comp) * SEG + 8


def buffer_rows(rows):
    return rows * 3 * SEG + 8


def zero_gaps(ref, rows):
    for i in range(rows * 3 + 1):
        ref[pl.ds(i * SEG, 8), :] = jnp.zeros((8, LANES), jnp.float32)


def load_coefficients(dep_ref, cor_ref, drag_ref, first, count, coef_ref, slot_of=None, turn=None, only=None):
    shift = lax.rem(128 - first + 128, 128)
    lane = lax.broadcasted_iota(jnp.int32, (GX, LANES), 1)
    inside = jnp.where(lane < GX, 1.0, 0.0).astype(jnp.float32)

    def rolled(ref, scale):
        wide = jnp.concatenate([ref[...].T, jnp.zeros((GX, LANES - GX), jnp.float32)], axis=1)
        return pltpu.roll(wide * scale, shift, 1)

    tables = {
        D: rolled(dep_ref, -0.5 * STEP),
        F: rolled(cor_ref, STEP),
        R: rolled(drag_ref, STEP),
        B: pltpu.roll(inside * (-0.5 * STEP), shift, 1),
    }
    if turn is not None:
        tables[F] = tables[F] * turn
    for j in only or range(count):
        slot = j if slot_of is None else slot_of(j)
        for kind, table in tables.items():
            coef_ref[slot, kind] = jnp.broadcast_to(table[:, j : j + 1], (GX, LANES))


def total(terms):
    terms = [t for t in terms if t is not None]
    if not terms:
        return None
    acc = terms[0]
    for t in terms[1:]:
        acc = acc + t
    return acc


def tendency(src, have, row, base, coef, slot, ghost=False, want=(0, 1, 2), turn=1):
    def get(r, c, shift=0):
        return src[pl.ds(at(r + base, c) + shift, GX), :]

    def diff_x(c):
        return get(row, c, 1) - get(row, c, -1)

    def diff_y(c):
        above, below = (row + 1, c) in have, (row - 1, c) in have
        if above and below:
            return get(row + 1, c) - get(row - 1, c)
        if above:
            return get(row + 1, c)
        if below:
            return -get(row - 1, c)
        return None

    half = coef[slot, B] if ghost else jnp.float32(-0.5 * STEP)
    center = [get(row, c) if (row, c) in have else None for c in range(3)]
    out = {}
    if 0 in want:
        s = total([diff_x(1) if center[1] is not None else None, diff_y(2)])
        out[0] = None if s is None else coef[slot, D] * s
    if 1 in want:
        dx = half * diff_x(0) if center[0] is not None else None
        spin = None if center[2] is None else (turn * coef[slot, F] if turn != 1 else coef[slot, F]) * center[2]
        drag = None if center[1] is None else -(coef[slot, R] * center[1])
        out[1] = total([dx, spin, drag])
    if 2 in want:
        dy = diff_y(0)
        dy = None if dy is None else half * dy
        spin = None if center[1] is None else (-turn * coef[slot, F]) * center[1]
        drag = None if center[2] is None else -(coef[slot, R] * center[2])
        out[2] = total([dy, spin, drag])
    return out


def powers(bufs, rows, base, coef, finish):
    have = {(r, c) for r in range(rows) for c in range(3)}
    for j, reach in ((1, 1), (2, 2), (3, 1)):
        new = set()
        for r in range(-reach, rows + reach):
            ghost = r < 0 or r >= rows
            want = (0, 2) if ghost and j == 3 else (0, 1, 2)
            out = tendency(bufs[j - 1], have, r, base, coef, r + 2, ghost, want)
            for c, v in out.items():
                if v is not None:
                    bufs[j][pl.ds(at(r + base, c), GX), :] = v if j == 1 else v * (1.0 / j)
                    new.add((r, c))
        have = new
    for r in range(rows):
        out = tendency(bufs[3], have, r, base, coef, r + 2)
        for c in range(3):
            finish(r, c, out[c] * 0.25)


FACT = [1.0, 1.0, 2.0, 6.0, 24.0]


def response(message, bufs, base, coef, slot_of, finish, turn=1, powers_in=(0, 1, 2, 3)):
    heights = {j: message(j, 0) for j in powers_in}
    norths = {j: message(j, 1) for j in powers_in}

    def force(m):
        weights = {j: FACT[j] / FACT[j + 1 + m] for j in powers_in if j <= 3 - m}
        if not weights:
            return None, None
        fh = total([w * heights[j] for j, w in weights.items()])
        fn = total([w * norths[j] for j, w in weights.items()])
        return -(coef[slot_of(0), D] * fn), (0.5 * STEP) * fh

    have = set()
    src = None
    for step, m in enumerate((3, 2, 1, 0)):
        new = set()
        for d in range(step + 1):
            out = {0: None, 1: None, 2: None}
            if src is not None:
                out = tendency(src, have, d, base, coef, slot_of(d), turn=turn)
            if d == 0:
                fh, fn = force(m)
                out[0] = total([out[0], fh])
                out[2] = total([out[2], fn])
            for c, v in out.items():
                if m == 0:
                    finish(d, c, v)
                elif v is not None:
                    bufs[step % 2][pl.ds(at(d + base, c), GX), :] = v
                    new.add((d, c))
        have, src = new, bufs[step % 2]


def rows_kernel(x_ref, dep, cor, drag, s00, s01, s10, s11, e0, e1, b0, b1, coef, v0, v1, v2, v3, acc):
    rows, base = 8, 2

    @pl.when(pl.program_id(0) == 0)
    def _():
        load_coefficients(dep, cor, drag, lax.axis_index("row") * rows - 2, rows + 4, coef)
        for ref in (v0, v1, v2, v3):
            zero_gaps(ref, rows + 4)

    for r in range(rows):
        for c in range(3):
            v0[pl.ds(at(r + base, c), GX), :] = x_ref[pl.ds((r * 3 + c) * GX, GX), :]

    def finish(r, c, v4):
        half, d = (0, r) if r < 4 else (1, 7 - r)
        place = half * 4 + (d + 2) % 4
        i = at(r + base, c)
        v = v4 + v3[pl.ds(i, GX), :] + v2[pl.ds(i, GX), :] + v1[pl.ds(i, GX), :] + v0[pl.ds(i, GX), :]
        acc[pl.ds((place * 3 + c) * GX, GX), :] = v

    powers((v0, v1, v2, v3), rows, base, coef, finish)

    def put(e_ref, b_ref, row):
        for j, ref in enumerate((v0, v1, v2, v3)):
            for i, c in enumerate((0, 2)):
                to = e_ref if j < 3 else b_ref
                to[pl.ds((j % 3 * 2 + i) * GX, GX), :] = ref[pl.ds(at(row + base, c), GX), :]

    half, part = 768, 384
    core = lax.axis_index("col") % 2

    @pl.when(core == 0)
    def _():
        s00[...] = acc[pl.ds(0, part), :]
        s01[...] = acc[pl.ds(part, part), :]
        s10[...] = acc[pl.ds(half, part), :]
        s11[...] = acc[pl.ds(half + part, part), :]
        put(e0, b0, 7)
        put(e1, b1, 0)

    @pl.when(core == 1)
    def _():
        s10[...] = acc[pl.ds(0, part), :]
        s11[...] = acc[pl.ds(part, part), :]
        s00[...] = acc[pl.ds(half, part), :]
        s01[...] = acc[pl.ds(half + part, part), :]
        put(e1, b1, 7)
        put(e0, b0, 0)


def whole(ref_shape):
    return pl.BlockSpec(ref_shape, lambda i, *_: tuple(0 for _ in ref_shape))


def vmem(rows, cols=LANES):
    return pltpu.VMEM((rows, cols), jnp.float32)


def shape(rows, cols):
    return jax.ShapeDtypeStruct((rows, cols), jnp.float32)


def params(mib):
    return pltpu.CompilerParams(vmem_limit_bytes=mib * MIB)


def lane_block(rows):
    return pl.BlockSpec((rows, LANES), lambda i, *_: (0, i))


def rows_step(block, fields):
    table = whole((GX, GX))
    buf = vmem(buffer_rows(12))
    return pl.pallas_call(
        rows_kernel,
        grid_spec=pltpu.PrefetchScalarGridSpec(
            num_scalar_prefetch=0,
            grid=(3,),
            in_specs=[lane_block(1536), table, table, table],
            out_specs=[lane_block(384)] * 6 + [lane_block(128)] * 2,
            scratch_shapes=[pltpu.VMEM((12, 4, GX, LANES), jnp.float32), buf, buf, buf, buf, vmem(1536)],
        ),
        out_shape=[shape(384, 384)] * 6 + [shape(128, 384)] * 2,
        compiler_params=params(58),
        name="rows_step",
    )(block, *fields)


def rows_response_kernel(scal, m0, m1, dep, cor, drag, *refs):
    outs, (coef, t0, t1) = refs[:-3], refs[-3:]
    half = scal[1]
    turn = 1.0 - 2.0 * half.astype(jnp.float32)

    @pl.when(pl.program_id(0) == 0)
    def _():
        load_coefficients(dep, cor, drag, scal[0], 4, coef, lambda j: jnp.where(half == 0, j, 3 - j), turn)
        for ref in (t0, t1):
            zero_gaps(ref, 4)

    for k, m_ref in enumerate((m0, m1)):

        def message(j, i, m_ref=m_ref):
            v = m_ref[pl.ds((j * 2 + i) * GX, GX), :]
            return v * turn if i == 1 else v

        def finish(d, c, v, k=k):
            v = jnp.zeros((GX, LANES), jnp.float32) if v is None else v
            outs[k + 2 * (d < 2)][pl.ds((d % 2 * 3 + c) * GX, GX), :] = v * turn if c == 2 else v

        response(message, (t0, t1), 0, coef, lambda d: d, finish, powers_in=(0, 1, 2))


def rows_response(scal, messages, fields):
    table = whole((GX, GX))
    buf = vmem(buffer_rows(4))
    return pl.pallas_call(
        rows_response_kernel,
        grid_spec=pltpu.PrefetchScalarGridSpec(
            num_scalar_prefetch=1,
            grid=(3,),
            in_specs=[lane_block(384)] * 2 + [table] * 3,
            out_specs=[lane_block(384)] * 4,
            scratch_shapes=[pltpu.VMEM((4, 4, GX, LANES), jnp.float32), buf, buf],
        ),
        out_shape=[shape(384, 384)] * 4,
        compiler_params=params(16),
        name="rows_response",
    )(scal, *messages, *fields)


def columns_kernel(scal, s0, s1, r0, r1, *refs):
    late, (dep, cor, drag, out, inner, outer, coef, v0, v1, v2, v3, near, extra) = refs[:-13], refs[-13:]
    rows, base = 4, 2
    half = scal[1]

    @pl.when(pl.program_id(0) == 0)
    def _():
        load_coefficients(dep, cor, drag, scal[0] - 2, rows + 4, coef)
        for ref in (v0, v1, v2, v3):
            zero_gaps(ref, rows + 4)

    if late:
        turn = 1.0 - 2.0 * half.astype(jnp.float32)

        @pl.when(pl.program_id(0) == 0)
        def _():
            load_coefficients(dep, cor, drag, scal[3], 4, near, lambda j: jnp.where(half == 0, j, 3 - j))
            for k in range(2):
                for t in range(3):
                    lanes = pl.ds(t * LANES, LANES)
                    extra[pl.ds(k * GX, GX), lanes] = near[0, D] * (late[k][pl.ds(GX, GX), lanes] * (-0.25 * turn))

        @pl.when(pl.program_id(0) == 1)
        def _():
            for k in range(2):
                extra[pl.ds(k * GX, GX), :] = late[k][pl.ds(0, GX), :] * (0.125 * STEP * turn)

        @pl.when(pl.program_id(0) == 2)
        def _():
            extra[...] = jnp.zeros_like(extra)

    for k, (s_ref, r_ref) in enumerate(((s0, r0), (s1, r1))):
        core = half if k == 0 else 1 - half
        start = pl.multiple_of(core * (2 * 3 * SEG), 8)
        for t in range(3):
            lanes = slice(t * LANES, (t + 1) * LANES)
            piece = s_ref[:, lanes] + r_ref[:, lanes]
            if late:
                more = extra[pl.ds(k * GX, GX), lanes]
                piece = jnp.concatenate([piece[:GX] + more, piece[GX:]], axis=0)
            piece = piece.T
            for i in range(2):
                seg = t * 2 + i
                place = pl.multiple_of(start + (base * 3 + seg) * SEG + 8, 8)
                v0[pl.ds(place, GX), :] = piece[i * GX : (i + 1) * GX, :]

    def finish(r, c, v4):
        i = at(r + base, c)
        v = v4 + v3[pl.ds(i, GX), :] + v2[pl.ds(i, GX), :] + v1[pl.ds(i, GX), :] + v0[pl.ds(i, GX), :]
        out[pl.ds((r * 3 + c) * GX, GX), :] = v

    powers((v0, v1, v2, v3), rows, base, coef, finish)

    def put(to, row):
        for j, ref in enumerate((v0, v1, v2, v3)):
            for i, c in enumerate((0, 2)):
                to[pl.ds((j * 2 + i) * GX, GX), :] = ref[pl.ds(at(row + base, c), GX), :]

    @pl.when(scal[2] == 0)
    def _():
        put(inner, rows - 1)
        put(outer, 0)

    @pl.when(scal[2] == 1)
    def _():
        put(inner, 0)
        put(outer, rows - 1)


def columns_step(scal, s0, s1, r0, r1, late, fields):
    table = whole((GX, GX))
    part = 768 // CHUNKS
    buf = vmem(buffer_rows(8))
    return pl.pallas_call(
        columns_kernel,
        grid_spec=pltpu.PrefetchScalarGridSpec(
            num_scalar_prefetch=1,
            grid=(part // LANES,),
            in_specs=[pl.BlockSpec((LANES, 384), lambda i, *_: (i, 0))] * 4
            + [whole((128, 384))] * len(late)
            + [table] * 3,
            out_specs=[lane_block(768), lane_block(512), lane_block(512)],
            scratch_shapes=[
                pltpu.VMEM((8, 4, GX, LANES), jnp.float32),
                *[buf] * 4,
                pltpu.VMEM((4, 4, GX, LANES), jnp.float32),
                vmem(2 * GX, 384),
            ],
        ),
        out_shape=[shape(768, part), shape(512, part), shape(512, part)],
        compiler_params=params(24),
        name="columns_step",
    )(scal, s0, s1, r0, r1, *late, *fields)


def columns_response_kernel(scal, own, inner, outer, dep, cor, drag, z0, z1, coef, t0, t1, acc):
    half = scal[1]

    @pl.when(pl.program_id(0) == 0)
    def _():
        load_coefficients(dep, cor, drag, scal[0], 4, coef)
        for ref in (t0, t1):
            zero_gaps(ref, 4)

    def message_left(j, i):
        place = pl.ds((j * 2 + i) * GX, GX)
        return jnp.where(scal[2] == 0, outer[place, :], inner[place, :])

    def finish_left(d, c, v):
        i = pl.ds((d * 3 + c) * GX, GX)
        acc[i, :] = own[i, :] if v is None else own[i, :] + v

    response(message_left, (t0, t1), 0, coef, lambda d: d, finish_left)

    def message_right(j, i):
        place = pl.ds((j * 2 + i) * GX, GX)
        v = jnp.where(scal[2] == 0, inner[place, :], outer[place, :])
        return -v if i == 1 else v

    def finish_right(d, c, v):
        i = pl.ds(((3 - d) * 3 + c) * GX, GX)
        if v is not None:
            acc[i, :] = acc[i, :] + (-v if c == 2 else v)

    response(message_right, (t0, t1), 0, coef, lambda d: 3 - d, finish_right, turn=-1)
    for k, z_ref in enumerate((z0, z1)):
        core = half if k == 0 else 1 - half
        for t in range(3):
            place = pl.multiple_of(core * 384 + t * LANES, LANES)
            z_ref[:, t * LANES : (t + 1) * LANES] = acc[pl.ds(place, LANES), :].T


def columns_response(scal, own, inner, outer, fields):
    table = whole((GX, GX))
    part = 768 // CHUNKS
    buf = vmem(buffer_rows(4))
    return pl.pallas_call(
        columns_response_kernel,
        grid_spec=pltpu.PrefetchScalarGridSpec(
            num_scalar_prefetch=1,
            grid=(part // LANES,),
            in_specs=[lane_block(768), lane_block(512), lane_block(512)] + [table] * 3,
            out_specs=[pl.BlockSpec((LANES, 384), lambda i, *_: (i, 0))] * 2,
            scratch_shapes=[pltpu.VMEM((4, 4, GX, LANES), jnp.float32), buf, buf, vmem(768)],
        ),
        out_shape=[shape(part, 384)] * 2,
        compiler_params=params(16),
        name="columns_response",
    )(scal, own, inner, outer, *fields)


def finish_kernel(scal, z0, z1, noise, *rest):
    out = rest[-1]
    k = pl.program_id(0)
    half = jnp.where(k == 0, scal[1], 1 - scal[1])

    def put(z, flip):
        for d in range(2):
            place = pl.ds((1 - d if flip else d) * 192, 192)
            out[place, :] = z[pl.ds(d * 192, 192), :] + noise[place, :]

    for i, z in enumerate((z0, z1)):
        for flip in (False, True):
            pl.when(jnp.logical_and(k == i, half == int(flip)))(functools.partial(put, z, flip))


def finish_step(scal, z0, z1, noise, near, out=None):
    def place(k, scal):
        half = jnp.where(k == 0, scal[1], 1 - scal[1])
        return (jnp.where(half == 0, 0, 3) if near else 1 + half, 0)

    full = pl.BlockSpec((384, 384), lambda k, scal: (0, 0))
    block = pl.BlockSpec((384, 384), place)
    extra = [] if out is None else [out]
    return pl.pallas_call(
        finish_kernel,
        grid_spec=pltpu.PrefetchScalarGridSpec(
            num_scalar_prefetch=1,
            grid=(2,),
            in_specs=[full, full, block] + [pl.BlockSpec(memory_space=pl.ANY)] * len(extra),
            out_specs=block,
        ),
        out_shape=shape(1536, 384),
        input_output_aliases={} if out is None else {4: 0},
        compiler_params=params(12),
        name="finish_step",
    )(scal, z0, z1, noise, *extra)


def permutations(rows, cols):
    def joint(r, z, a, b):
        return r * cols + z * 4 + a * 2 + b

    split, boundary, back = [[], []], [[], []], [[], []]
    for k in range(2):
        for r in range(rows):
            for z in range(cols // 4):
                for lo in range(2):
                    for core in range(2):
                        me = joint(r, z, lo, core)
                        split[k].append((me, joint(r, z, core ^ k, lo)))
                        if core == k and r + 1 < rows:
                            boundary[k].append((me, joint(r + 1, z, 0, lo)))
                        if core != k and r > 0:
                            boundary[k].append((me, joint(r - 1, z, 1, lo)))
                        back[k].append((me, joint(r, z, core, lo ^ k)))
    inner = [(i, i ^ 1) for i in range(cols)]
    outer = []
    for z in range(cols // 4 - 1):
        for p in range(2):
            a, b = z * 4 + p * 2 + 1, (z + 1) * 4 + p * 2
            outer += [(a, b), (b, a)]
    return split, boundary, back, inner, outer


def shards(covariance, process_noise, depth_field, coriolis, drag_rate):
    fields = (depth_field, coriolis, drag_rate)
    rows, cols = lax.axis_size("row"), lax.axis_size("col")
    split, boundary, back, inner, outer = permutations(rows, cols)
    row, col = lax.axis_index("row"), lax.axis_index("col")
    z, second, core = col // 4, (col // 2) % 2, col % 2
    both = ("row", "col")

    def send(pair, pairs):
        return [lax.ppermute(v, both, pairs[k]) for k, v in enumerate(pair)]

    s00, s01, s10, s11, e0, e1, b0, b1 = rows_step(covariance, fields)
    early = send((e0, e1), boundary)
    far = send((s00, s10), split)
    late = send((b0, b1), boundary)
    near = [lax.ppermute(s01, both, split[0])]
    far[1], s11 = lax.optimization_barrier((far[1], s11))
    near.append(lax.ppermute(s11, both, split[1]))
    rscal = jnp.stack([row * 8 + second * 4, second]).astype(jnp.int32)
    cscal = jnp.stack([(z * 2 + core) * 4, second, core, row * 8 + second * 4]).astype(jnp.int32)
    fscal = jnp.stack([row, core]).astype(jnp.int32)
    r02, r12, r00, r10 = rows_response(rscal, early, fields)
    result = None
    for chunk, halves, moved, rest in ((0, far, (r02, r12), ()), (1, near, (r00, r10), late)):
        own, inside, outside = columns_step(cscal, *halves, *moved, rest, fields)
        outside = lax.ppermute(outside, "col", outer)
        inside = lax.ppermute(inside, "col", inner)
        ready = send(columns_response(cscal, own, inside, outside, fields), back)
        result = finish_step(fscal, *ready, process_noise, chunk == 1, result)
    return result


def solution(mesh):
    return jax.shard_map(
        shards,
        mesh=mesh,
        in_specs=(P("row", "col"), P("row", "col"), P(), P(), P()),
        out_specs=P("row", "col"),
        check_vma=False,
    )
```

```python
import functools

import jax
import jax.numpy as jnp
from jax import lax
from jax.experimental import pallas as pl
from jax.experimental.pallas import tpu as pltpu
from jax.sharding import PartitionSpec as P

GX = 64
STEP = 0.9
SEG = 72
LANES = 128
CHUNKS = 2
D, F, R, B = 0, 1, 2, 3
MIB = 1024 * 1024


def at(row, comp):
    return (row * 3 + comp) * SEG + 8


def buffer_rows(rows):
    return rows * 3 * SEG + 8


def zero_gaps(ref, rows):
    for i in range(rows * 3 + 1):
        ref[pl.ds(i * SEG, 8), :] = jnp.zeros((8, LANES), jnp.float32)


def load_coefficients(dep_ref, cor_ref, drag_ref, first, count, coef_ref, slot_of=None, turn=None, only=None):
    shift = lax.rem(128 - first + 128, 128)
    lane = lax.broadcasted_iota(jnp.int32, (GX, LANES), 1)
    inside = jnp.where(lane < GX, 1.0, 0.0).astype(jnp.float32)

    def rolled(ref, scale):
        wide = jnp.concatenate([ref[...].T, jnp.zeros((GX, LANES - GX), jnp.float32)], axis=1)
        return pltpu.roll(wide * scale, shift, 1)

    tables = {
        D: rolled(dep_ref, -0.5 * STEP),
        F: rolled(cor_ref, STEP),
        R: rolled(drag_ref, STEP),
        B: pltpu.roll(inside * (-0.5 * STEP), shift, 1),
    }
    if turn is not None:
        tables[F] = tables[F] * turn
    for j in only or range(count):
        slot = j if slot_of is None else slot_of(j)
        for kind, table in tables.items():
            coef_ref[slot, kind] = jnp.broadcast_to(table[:, j : j + 1], (GX, LANES))


def total(terms):
    terms = [t for t in terms if t is not None]
    if not terms:
        return None
    acc = terms[0]
    for t in terms[1:]:
        acc = acc + t
    return acc


def tendency(src, have, row, base, coef, slot, ghost=False, want=(0, 1, 2), turn=1):
    def get(r, c, shift=0):
        return src[pl.ds(at(r + base, c) + shift, GX), :]

    def diff_x(c):
        return get(row, c, 1) - get(row, c, -1)

    def diff_y(c):
        above, below = (row + 1, c) in have, (row - 1, c) in have
        if above and below:
            return get(row + 1, c) - get(row - 1, c)
        if above:
            return get(row + 1, c)
        if below:
            return -get(row - 1, c)
        return None

    half = coef[slot, B] if ghost else jnp.float32(-0.5 * STEP)
    center = [get(row, c) if (row, c) in have else None for c in range(3)]
    out = {}
    if 0 in want:
        s = total([diff_x(1) if center[1] is not None else None, diff_y(2)])
        out[0] = None if s is None else coef[slot, D] * s
    if 1 in want:
        dx = half * diff_x(0) if center[0] is not None else None
        spin = None if center[2] is None else (turn * coef[slot, F] if turn != 1 else coef[slot, F]) * center[2]
        drag = None if center[1] is None else -(coef[slot, R] * center[1])
        out[1] = total([dx, spin, drag])
    if 2 in want:
        dy = diff_y(0)
        dy = None if dy is None else half * dy
        spin = None if center[1] is None else (-turn * coef[slot, F]) * center[1]
        drag = None if center[2] is None else -(coef[slot, R] * center[2])
        out[2] = total([dy, spin, drag])
    return out


def powers(bufs, rows, base, coef, finish):
    have = {(r, c) for r in range(rows) for c in range(3)}
    for j, reach in ((1, 1), (2, 2), (3, 1)):
        new = set()
        for r in range(-reach, rows + reach):
            ghost = r < 0 or r >= rows
            want = (0, 2) if ghost and j == 3 else (0, 1, 2)
            out = tendency(bufs[j - 1], have, r, base, coef, r + 2, ghost, want)
            for c, v in out.items():
                if v is not None:
                    bufs[j][pl.ds(at(r + base, c), GX), :] = v if j == 1 else v * (1.0 / j)
                    new.add((r, c))
        have = new
    for r in range(rows):
        out = tendency(bufs[3], have, r, base, coef, r + 2)
        for c in range(3):
            finish(r, c, out[c] * 0.25)


FACT = [1.0, 1.0, 2.0, 6.0, 24.0]


def response(message, bufs, base, coef, slot_of, finish, turn=1, powers_in=(0, 1, 2, 3)):
    heights = {j: message(j, 0) for j in powers_in}
    norths = {j: message(j, 1) for j in powers_in}

    def force(m):
        weights = {j: FACT[j] / FACT[j + 1 + m] for j in powers_in if j <= 3 - m}
        if not weights:
            return None, None
        fh = total([w * heights[j] for j, w in weights.items()])
        fn = total([w * norths[j] for j, w in weights.items()])
        return -(coef[slot_of(0), D] * fn), (0.5 * STEP) * fh

    have = set()
    src = None
    for step, m in enumerate((3, 2, 1, 0)):
        new = set()
        for d in range(step + 1):
            out = {0: None, 1: None, 2: None}
            if src is not None:
                out = tendency(src, have, d, base, coef, slot_of(d), turn=turn)
            if d == 0:
                fh, fn = force(m)
                out[0] = total([out[0], fh])
                out[2] = total([out[2], fn])
            for c, v in out.items():
                if m == 0:
                    finish(d, c, v)
                elif v is not None:
                    bufs[step % 2][pl.ds(at(d + base, c), GX), :] = v
                    new.add((d, c))
        have, src = new, bufs[step % 2]


def rows_kernel(x_ref, dep, cor, drag, s00, s01, s10, s11, e0, e1, b0, b1, coef, v0, v1, v2, v3, acc):
    rows, base = 8, 2

    @pl.when(pl.program_id(0) == 0)
    def _():
        load_coefficients(dep, cor, drag, lax.axis_index("row") * rows - 2, rows + 4, coef)
        for ref in (v0, v1, v2, v3):
            zero_gaps(ref, rows + 4)

    for r in range(rows):
        for c in range(3):
            v0[pl.ds(at(r + base, c), GX), :] = x_ref[pl.ds((r * 3 + c) * GX, GX), :]

    def finish(r, c, v4):
        half, d = (0, r) if r < 4 else (1, 7 - r)
        place = half * 4 + (d + 2) % 4
        i = at(r + base, c)
        v = v4 + v3[pl.ds(i, GX), :] + v2[pl.ds(i, GX), :] + v1[pl.ds(i, GX), :] + v0[pl.ds(i, GX), :]
        acc[pl.ds((place * 3 + c) * GX, GX), :] = v

    powers((v0, v1, v2, v3), rows, base, coef, finish)

    def put(e_ref, b_ref, row):
        for j, ref in enumerate((v0, v1, v2, v3)):
            for i, c in enumerate((0, 2)):
                to = e_ref if j < 3 else b_ref
                to[pl.ds((j % 3 * 2 + i) * GX, GX), :] = ref[pl.ds(at(row + base, c), GX), :]

    half, part = 768, 384
    core = lax.axis_index("col") % 2

    @pl.when(core == 0)
    def _():
        s00[...] = acc[pl.ds(0, part), :]
        s01[...] = acc[pl.ds(part, part), :]
        s10[...] = acc[pl.ds(half, part), :]
        s11[...] = acc[pl.ds(half + part, part), :]
        put(e0, b0, 7)
        put(e1, b1, 0)

    @pl.when(core == 1)
    def _():
        s10[...] = acc[pl.ds(0, part), :]
        s11[...] = acc[pl.ds(part, part), :]
        s00[...] = acc[pl.ds(half, part), :]
        s01[...] = acc[pl.ds(half + part, part), :]
        put(e1, b1, 7)
        put(e0, b0, 0)


def whole(ref_shape):
    return pl.BlockSpec(ref_shape, lambda i, *_: tuple(0 for _ in ref_shape))


def vmem(rows, cols=LANES):
    return pltpu.VMEM((rows, cols), jnp.float32)


def shape(rows, cols):
    return jax.ShapeDtypeStruct((rows, cols), jnp.float32)


def params(mib):
    return pltpu.CompilerParams(vmem_limit_bytes=mib * MIB)


def lane_block(rows):
    return pl.BlockSpec((rows, LANES), lambda i, *_: (0, i))


def stacked(rows):
    return pl.BlockSpec((rows, LANES), lambda i, *_: (i, 0))


def rows_step(block, fields):
    table = whole((GX, GX))
    buf = vmem(buffer_rows(12))
    return pl.pallas_call(
        rows_kernel,
        grid_spec=pltpu.PrefetchScalarGridSpec(
            num_scalar_prefetch=0,
            grid=(3,),
            in_specs=[lane_block(1536), table, table, table],
            out_specs=[lane_block(384)] * 6 + [lane_block(128)] * 2,
            scratch_shapes=[pltpu.VMEM((12, 4, GX, LANES), jnp.float32), buf, buf, buf, buf, vmem(1536)],
        ),
        out_shape=[shape(384, 384)] * 6 + [shape(128, 384)] * 2,
        compiler_params=params(58),
        name="rows_step",
    )(block, *fields)


def rows_response_kernel(scal, m0, m1, dep, cor, drag, *refs):
    outs, (coef, t0, t1) = refs[:-3], refs[-3:]
    half = scal[1]
    turn = 1.0 - 2.0 * half.astype(jnp.float32)

    @pl.when(pl.program_id(0) == 0)
    def _():
        load_coefficients(dep, cor, drag, scal[0], 4, coef, lambda j: jnp.where(half == 0, j, 3 - j), turn)
        for ref in (t0, t1):
            zero_gaps(ref, 4)

    for k, m_ref in enumerate((m0, m1)):

        def message(j, i, m_ref=m_ref):
            v = m_ref[pl.ds((j * 2 + i) * GX, GX), :]
            return v * turn if i == 1 else v

        def finish(d, c, v, k=k):
            v = jnp.zeros((GX, LANES), jnp.float32) if v is None else v
            outs[k + 2 * (d < 2)][pl.ds((d % 2 * 3 + c) * GX, GX), :] = v * turn if c == 2 else v

        response(message, (t0, t1), 0, coef, lambda d: d, finish, powers_in=(0, 1, 2))


def rows_response(scal, messages, fields):
    table = whole((GX, GX))
    buf = vmem(buffer_rows(4))
    return pl.pallas_call(
        rows_response_kernel,
        grid_spec=pltpu.PrefetchScalarGridSpec(
            num_scalar_prefetch=1,
            grid=(3,),
            in_specs=[lane_block(384)] * 2 + [table] * 3,
            out_specs=[lane_block(384)] * 4,
            scratch_shapes=[pltpu.VMEM((4, 4, GX, LANES), jnp.float32), buf, buf],
        ),
        out_shape=[shape(384, 384)] * 4,
        compiler_params=params(16),
        name="rows_response",
    )(scal, *messages, *fields)


def columns_kernel(scal, s0, s1, r0, r1, *refs):
    late, (dep, cor, drag, out, inner, outer, coef, v0, v1, v2, v3, near, extra) = refs[:-13], refs[-13:]
    rows, base = 4, 2
    half = scal[1]

    @pl.when(pl.program_id(0) == 0)
    def _():
        load_coefficients(dep, cor, drag, scal[0] - 2, rows + 4, coef)
        for ref in (v0, v1, v2, v3):
            zero_gaps(ref, rows + 4)

    if late:
        turn = 1.0 - 2.0 * half.astype(jnp.float32)

        @pl.when(pl.program_id(0) == 0)
        def _():
            load_coefficients(dep, cor, drag, scal[3], 4, near, lambda j: jnp.where(half == 0, j, 3 - j))
            for k in range(2):
                for t in range(3):
                    lanes = pl.ds(t * LANES, LANES)
                    extra[pl.ds(k * GX, GX), lanes] = near[0, D] * (late[k][pl.ds(GX, GX), lanes] * (-0.25 * turn))

        @pl.when(pl.program_id(0) == 1)
        def _():
            for k in range(2):
                extra[pl.ds(k * GX, GX), :] = late[k][pl.ds(0, GX), :] * (0.125 * STEP * turn)

        @pl.when(pl.program_id(0) == 2)
        def _():
            extra[...] = jnp.zeros_like(extra)

    for k, (s_ref, r_ref) in enumerate(((s0, r0), (s1, r1))):
        core = half if k == 0 else 1 - half
        start = pl.multiple_of(core * (2 * 3 * SEG), 8)
        for t in range(3):
            lanes = slice(t * LANES, (t + 1) * LANES)
            piece = s_ref[:, lanes] + r_ref[:, lanes]
            if late:
                more = extra[pl.ds(k * GX, GX), lanes]
                piece = jnp.concatenate([piece[:GX] + more, piece[GX:]], axis=0)
            piece = piece.T
            for i in range(2):
                seg = t * 2 + i
                place = pl.multiple_of(start + (base * 3 + seg) * SEG + 8, 8)
                v0[pl.ds(place, GX), :] = piece[i * GX : (i + 1) * GX, :]

    def finish(r, c, v4):
        i = at(r + base, c)
        v = v4 + v3[pl.ds(i, GX), :] + v2[pl.ds(i, GX), :] + v1[pl.ds(i, GX), :] + v0[pl.ds(i, GX), :]
        out[pl.ds((r * 3 + c) * GX, GX), :] = v

    powers((v0, v1, v2, v3), rows, base, coef, finish)

    def put(to, row):
        for j, ref in enumerate((v0, v1, v2, v3)):
            for i, c in enumerate((0, 2)):
                to[pl.ds((j * 2 + i) * GX, GX), :] = ref[pl.ds(at(row + base, c), GX), :]

    @pl.when(scal[2] == 0)
    def _():
        put(inner, rows - 1)
        put(outer, 0)

    @pl.when(scal[2] == 1)
    def _():
        put(inner, 0)
        put(outer, rows - 1)


def columns_step(scal, s0, s1, r0, r1, late, fields):
    table = whole((GX, GX))
    part = 768 // CHUNKS
    buf = vmem(buffer_rows(8))
    return pl.pallas_call(
        columns_kernel,
        grid_spec=pltpu.PrefetchScalarGridSpec(
            num_scalar_prefetch=1,
            grid=(part // LANES,),
            in_specs=[pl.BlockSpec((LANES, 384), lambda i, *_: (i, 0))] * 4
            + [whole((128, 384))] * len(late)
            + [table] * 3,
            out_specs=[stacked(768), stacked(512), stacked(512)],
            scratch_shapes=[
                pltpu.VMEM((8, 4, GX, LANES), jnp.float32),
                *[buf] * 4,
                pltpu.VMEM((4, 4, GX, LANES), jnp.float32),
                vmem(2 * GX, 384),
            ],
        ),
        out_shape=[shape(part * 6, LANES), shape(part * 4, LANES), shape(part * 4, LANES)],
        compiler_params=params(24),
        name="columns_step",
    )(scal, s0, s1, r0, r1, *late, *fields)


def columns_response_kernel(scal, own, inner, outer, dep, cor, drag, z0, z1, coef, t0, t1, acc):
    half = scal[1]

    @pl.when(pl.program_id(0) == 0)
    def _():
        load_coefficients(dep, cor, drag, scal[0], 4, coef)
        for ref in (t0, t1):
            zero_gaps(ref, 4)

    def message_left(j, i):
        place = pl.ds((j * 2 + i) * GX, GX)
        return jnp.where(scal[2] == 0, outer[place, :], inner[place, :])

    def finish_left(d, c, v):
        i = pl.ds((d * 3 + c) * GX, GX)
        acc[i, :] = own[i, :] if v is None else own[i, :] + v

    response(message_left, (t0, t1), 0, coef, lambda d: d, finish_left)

    def message_right(j, i):
        place = pl.ds((j * 2 + i) * GX, GX)
        v = jnp.where(scal[2] == 0, inner[place, :], outer[place, :])
        return -v if i == 1 else v

    def finish_right(d, c, v):
        i = pl.ds(((3 - d) * 3 + c) * GX, GX)
        if v is not None:
            acc[i, :] = acc[i, :] + (-v if c == 2 else v)

    response(message_right, (t0, t1), 0, coef, lambda d: 3 - d, finish_right, turn=-1)
    for k, z_ref in enumerate((z0, z1)):
        core = half if k == 0 else 1 - half
        for t in range(3):
            place = pl.multiple_of(core * 384 + t * LANES, LANES)
            z_ref[:, t * LANES : (t + 1) * LANES] = acc[pl.ds(place, LANES), :].T


def columns_response(scal, own, inner, outer, fields):
    table = whole((GX, GX))
    part = 768 // CHUNKS
    buf = vmem(buffer_rows(4))
    return pl.pallas_call(
        columns_response_kernel,
        grid_spec=pltpu.PrefetchScalarGridSpec(
            num_scalar_prefetch=1,
            grid=(part // LANES,),
            in_specs=[stacked(768), stacked(512), stacked(512)] + [table] * 3,
            out_specs=[pl.BlockSpec((LANES, 384), lambda i, *_: (i, 0))] * 2,
            scratch_shapes=[pltpu.VMEM((4, 4, GX, LANES), jnp.float32), buf, buf, vmem(768)],
        ),
        out_shape=[shape(part, 384)] * 2,
        compiler_params=params(16),
        name="columns_response",
    )(scal, own, inner, outer, *fields)


def finish_kernel(scal, z0, z1, noise, *rest):
    out = rest[-1]
    k = pl.program_id(0)
    half = jnp.where(k == 0, scal[1], 1 - scal[1])

    def put(z, flip):
        for d in range(2):
            place = pl.ds((1 - d if flip else d) * 192, 192)
            out[place, :] = z[pl.ds(d * 192, 192), :] + noise[place, :]

    for i, z in enumerate((z0, z1)):
        for flip in (False, True):
            pl.when(jnp.logical_and(k == i, half == int(flip)))(functools.partial(put, z, flip))


def finish_step(scal, z0, z1, noise, near, out=None):
    def place(k, scal):
        half = jnp.where(k == 0, scal[1], 1 - scal[1])
        return (jnp.where(half == 0, 0, 3) if near else 1 + half, 0)

    full = pl.BlockSpec((384, 384), lambda k, scal: (0, 0))
    block = pl.BlockSpec((384, 384), place)
    extra = [] if out is None else [out]
    return pl.pallas_call(
        finish_kernel,
        grid_spec=pltpu.PrefetchScalarGridSpec(
            num_scalar_prefetch=1,
            grid=(2,),
            in_specs=[full, full, block] + [pl.BlockSpec(memory_space=pl.ANY)] * len(extra),
            out_specs=block,
        ),
        out_shape=shape(1536, 384),
        input_output_aliases={} if out is None else {4: 0},
        compiler_params=params(12),
        name="finish_step",
    )(scal, z0, z1, noise, *extra)


def permutations(rows, cols):
    def joint(r, z, a, b):
        return r * cols + z * 4 + a * 2 + b

    split, boundary, back = [[], []], [[], []], [[], []]
    for k in range(2):
        for r in range(rows):
            for z in range(cols // 4):
                for lo in range(2):
                    for core in range(2):
                        me = joint(r, z, lo, core)
                        split[k].append((me, joint(r, z, core ^ k, lo)))
                        if core == k and r + 1 < rows:
                            boundary[k].append((me, joint(r + 1, z, 0, lo)))
                        if core != k and r > 0:
                            boundary[k].append((me, joint(r - 1, z, 1, lo)))
                        back[k].append((me, joint(r, z, core, lo ^ k)))
    inner = [(i, i ^ 1) for i in range(cols)]
    outer = []
    for z in range(cols // 4 - 1):
        for p in range(2):
            a, b = z * 4 + p * 2 + 1, (z + 1) * 4 + p * 2
            outer += [(a, b), (b, a)]
    return split, boundary, back, inner, outer


def shards(covariance, process_noise, depth_field, coriolis, drag_rate):
    fields = (depth_field, coriolis, drag_rate)
    rows, cols = lax.axis_size("row"), lax.axis_size("col")
    split, boundary, back, inner, outer = permutations(rows, cols)
    row, col = lax.axis_index("row"), lax.axis_index("col")
    z, second, core = col // 4, (col // 2) % 2, col % 2
    both = ("row", "col")

    def send(pair, pairs):
        return [lax.ppermute(v, both, pairs[k]) for k, v in enumerate(pair)]

    s00, s01, s10, s11, e0, e1, b0, b1 = rows_step(covariance, fields)
    early = send((e0, e1), boundary)
    far = send((s00, s10), split)
    late = send((b0, b1), boundary)
    near = [lax.ppermute(s01, both, split[0])]
    far[1], s11 = lax.optimization_barrier((far[1], s11))
    near.append(lax.ppermute(s11, both, split[1]))
    rscal = jnp.stack([row * 8 + second * 4, second]).astype(jnp.int32)
    cscal = jnp.stack([(z * 2 + core) * 4, second, core, row * 8 + second * 4]).astype(jnp.int32)
    fscal = jnp.stack([row, core]).astype(jnp.int32)
    r02, r12, r00, r10 = rows_response(rscal, early, fields)
    result = None
    for chunk, halves, moved, rest in ((0, far, (r02, r12), ()), (1, near, (r00, r10), late)):
        own, inside, outside = columns_step(cscal, *halves, *moved, rest, fields)
        outside = lax.ppermute(outside, "col", outer)
        inside = lax.ppermute(inside, "col", inner)
        ready = send(columns_response(cscal, own, inside, outside, fields), back)
        result = finish_step(fscal, *ready, process_noise, chunk == 1, result)
    return result


def solution(mesh):
    return jax.shard_map(
        shards,
        mesh=mesh,
        in_specs=(P("row", "col"), P("row", "col"), P(), P(), P()),
        out_specs=P("row", "col"),
        check_vma=False,
    )
```
